512 devices in a mesh: band: 8 (over z), pw: 64 (over y, x, core).
Axes of the slice: x: 4, y: 8, z: 8, core: 2. Of those that a mesh axis runs over, the one named last changes fastest.
Arguments:
- basis_re: float32 [8, 8, 8, 16384], P(None, None, 'band', 'pw'), may hold values from -24 to 24
- basis_im: float32 [8, 8, 8, 16384], P(None, None, 'band', 'pw'), may hold values from -24 to 24
- potential: float32 [192, 192, 192], P('pw'), may hold values from -15 to 15
- kinetic: float32 [8, 16384], P(None, 'pw'), may hold values from 0 to 30
- form_factors: float32 [8, 8, 16384], P(None, None, 'pw'), may hold values from -12 to 12
- channel_strength: float32 [8], replicated, may hold values from -4 to 4
- sphere_map: int32 [8, 16384], P(None, 'pw'), may hold values from 0 to 6143, as said below
- column_map: int32 [2048], replicated, may hold values from 0 to 36863, as said below
- atom_sites: int32 [3, 512], replicated, may hold values from 0 to 191
Outputs:
- next_re: float32 [8, 8, 16384], P(None, 'band', 'pw')
- next_im: float32 [8, 8, 16384], P(None, 'band', 'pw')
- coeffs_re: float32 [8, 8, 8], replicated
- coeffs_im: float32 [8, 8, 8], replicated
- chol_re: float32 [8, 8], replicated
- chol_im: float32 [8, 8], replicated
The draws below stay inside these ranges and needn't reach their ends.
Inputs may be any that keep to these rules, and one draw needn't show every extreme that they name: `sphere_map`: within each group of 256 consecutive values of the second index, the entries over both indices are distinct. `column_map`: all entries are distinct.
All inputs are finite; a program needn't handle non-finite values.
Results may differ from the reference program's by a relative error of at most 0.0015.
The reference program's roundings to bfloat16 on the way count: a program that leaves them out, or rounds other values in their place, can miss the bound.
Values sent between devices are 32-bit elements; how exact they have to be, the bound alone decides.
No kernel may reach another device: no remote copies, remote signals or barrier semaphores. Data moves between devices by JAX's collectives and lax.ppermute only.
A program may use at most 128 MiB of HBM per device.

```python
import math
import jax
import jax.numpy as jnp
from jax import lax

GRID = 192
ROWS_DEV = 256
BLOCKS = 8
ATOMS = 512
CHANNELS = 8
SLAB = 8
PW_SUB = 16384
PWAVES = 131072
COL_DEV = 32
COLUMNS = 2048
N_BAND = 8


def pick_distinct(key, span, count):
    middle = jax.random.permutation(key, span - 2)[:count - 2].astype(jnp.int32) + 1
    chosen = jnp.concatenate([jnp.array([0, span - 1], dtype=jnp.int32), middle])
    return chosen[jax.random.permutation(jax.random.fold_in(key, 5), count)]


def band_scales(key):
    low = math.log(0.4)
    high = math.log(4.0)
    return jnp.exp(jax.random.uniform(jax.random.fold_in(key, 97), (1, SLAB, 1, 1), jnp.float32, low, high))


def draw_basis_re(key, part):
    scales = band_scales(key)
    key = jax.random.fold_in(key, 1)
    shape = (BLOCKS, SLAB, PWAVES // PW_SUB, PW_SUB)
    own_key, shared_key = jax.random.split(key)
    noise = jnp.clip(jax.random.normal(own_key, shape, jnp.float32), -4.0, 4.0)
    common = 0.5 * jnp.clip(jax.random.normal(shared_key, (1,) + shape[1:], jnp.float32), -4.0, 4.0)
    return scales * (noise + common)


def draw_basis_im(key, part):
    scales = band_scales(key)
    key = jax.random.fold_in(key, 2)
    shape = (BLOCKS, SLAB, PWAVES // PW_SUB, PW_SUB)
    own_key, shared_key = jax.random.split(key)
    noise = jnp.clip(jax.random.normal(own_key, shape, jnp.float32), -4.0, 4.0)
    common = 0.5 * jnp.clip(jax.random.normal(shared_key, (1,) + shape[1:], jnp.float32), -4.0, 4.0)
    return scales * (noise + common)


def draw_sphere_map(key, part):
    key = jax.random.fold_in(key, 3)
    groups = PW_SUB // ROWS_DEV
    subs = PWAVES // PW_SUB
    keys = jax.random.split(key, groups)

    def one_group(group_key):
        return pick_distinct(group_key, COL_DEV * GRID, subs * ROWS_DEV)
    cells = jax.vmap(one_group)(keys)
    return cells.reshape(groups, subs, ROWS_DEV).transpose(1, 0, 2).reshape(subs, PW_SUB)


def draw_kinetic(key, part):
    key = jax.random.fold_in(key, 4)
    subs = PWAVES // PW_SUB
    ramp = 1.0 + 2.0 * jnp.arange(PWAVES, dtype=jnp.float32).reshape(subs, PW_SUB) / PWAVES
    base = jnp.exp(jax.random.uniform(key, (subs, PW_SUB), jnp.float32, math.log(0.1), math.log(10.0)))
    return base * ramp


def draw_form_factors(key, part):
    key = jax.random.fold_in(key, 6)
    subs = PWAVES // PW_SUB
    shape = (CHANNELS, subs, PW_SUB)
    ramp = 1.0 + 2.0 * jnp.arange(PW_SUB, dtype=jnp.float32) / PW_SUB
    base = jnp.clip(jax.random.normal(key, shape, jnp.float32), -4.0, 4.0)
    return base * ramp


def draw_column_map(key, part):
    key = jax.random.fold_in(key, 7)
    return pick_distinct(key, GRID * GRID, COLUMNS)


def touch_ends(result, key, smallest, high):
    spot = [jax.random.randint(jax.random.fold_in(key, axis), (), 0, length) for axis, length in enumerate(result.shape)]
    longest = result.shape.index(max(result.shape))
    neighbour = spot[:longest] + [(spot[longest] + 1) % result.shape[longest]] + spot[longest + 1:]
    return result.at[tuple(spot)].set(smallest).at[tuple(neighbour)].set(high)


def levels(key, dims, shards, smallest, high):
    loudness, own = 1.0, jax.random.fold_in(key, 6)
    for position, parts in shards:
        heights = jnp.exp(jax.random.uniform(jax.random.fold_in(own, position), (parts,), jnp.float32, smallest / len(shards), high / len(shards)))
        loudness = loudness * jnp.repeat(heights, dims[position] // parts).reshape([-1 if axis == position else 1 for axis in range(len(dims))])
    return loudness


def centred(rng, shape, scale, reach, cuts=(), kind=jnp.bfloat16):
    loudness = levels(rng, shape, cuts, -0.22, 0.18) if cuts else 1.0
    values = jax.random.normal(rng, shape, jnp.float32) * scale * loudness
    return jnp.minimum(jnp.maximum(values, -reach), reach).astype(kind)


def setup_inputs(seed: int = 0) -> dict:
    key_list = jax.random.split(jax.random.key(seed), 10)
    return {
        "basis_re": draw_basis_re(jax.random.fold_in(key_list[9], 71), 0),
        "basis_im": draw_basis_im(jax.random.fold_in(key_list[9], 71), 0),
        "potential": centred(key_list[2], (GRID, GRID, GRID), 3.0, 15.0, ((0, 64),), jnp.float32),
        "kinetic": draw_kinetic(jax.random.fold_in(key_list[9], 71), 0),
        "form_factors": draw_form_factors(jax.random.fold_in(key_list[9], 71), 0),
        "channel_strength": jnp.clip(jax.random.uniform(key_list[5], (CHANNELS,), jnp.float32, -4.0, 4.0), -4.0, 4.0),
        "sphere_map": draw_sphere_map(jax.random.fold_in(key_list[9], 71), 0),
        "column_map": draw_column_map(jax.random.fold_in(key_list[9], 71), 0),
        "atom_sites": touch_ends(jax.random.randint(key_list[8], (3, ATOMS), 0, GRID), jax.random.fold_in(key_list[8], 1), 0, GRID - 1).astype(jnp.int32),
    }


exact_mode = lax.Precision.HIGHEST

def contract(left, right, left_dim, right_dim):
    return lax.dot_general(left, right, (((left_dim,), (right_dim,)), ((), ())), precision=exact_mode, preferred_element_type=jnp.float32)

def conj_product(left_re, left_im, right_re, right_im, left_dim, scale):
    real = contract(left_re, right_re, left_dim, left_dim) + contract(left_im, right_im, left_dim, left_dim)
    imag = contract(left_re, right_im, left_dim, left_dim) - contract(left_im, right_re, left_dim, left_dim)
    return (real * scale, imag * scale)

def phase_table(depth, x_index, y_index, atom_sites, grid):
    turns = (depth[:, None] * atom_sites[0][None, :] + x_index[:, None] * atom_sites[1][None, :] + y_index[:, None] * atom_sites[2][None, :]) % grid
    angle = turns.astype(jnp.float32) * (2.0 * math.pi / grid)
    return jnp.concatenate([jnp.cos(angle).astype(jnp.bfloat16), jnp.sin(angle).astype(jnp.bfloat16)], 1)

def weigh(form, wave_re, wave_im):
    channels = form.shape[0]
    bands = wave_re.shape[0]
    part_re = (form[:, None, :] * wave_re[None]).reshape(channels * bands, -1)
    part_im = (form[:, None, :] * wave_im[None]).reshape(channels * bands, -1)
    return jnp.concatenate([part_re.astype(jnp.bfloat16), part_im.astype(jnp.bfloat16)], 0)

def project(weighted, phase):
    half = weighted.shape[0] // 2
    atoms = phase.shape[1] // 2
    mixed = jnp.dot(weighted, phase, preferred_element_type=jnp.float32)
    return (mixed[:half, :atoms] - mixed[half:, atoms:], mixed[:half, atoms:] + mixed[half:, :atoms])

def apply_back(form, sum_re, sum_im, strength, phase, root_waves):
    channels = form.shape[0]
    bands = sum_re.shape[0] // channels
    factor = jnp.repeat(strength, bands)[:, None]
    scaled_re = (factor * (sum_re / root_waves) / root_waves).astype(jnp.bfloat16)
    scaled_im = (factor * (sum_im / root_waves) / root_waves).astype(jnp.bfloat16)
    stacked = jnp.concatenate([jnp.concatenate([scaled_re, scaled_im], 1), jnp.concatenate([scaled_im, -scaled_re], 1)], 0)
    mixed = lax.dot_general(stacked, phase, (((1,), (1,)), ((), ())), preferred_element_type=jnp.float32)
    back_re = mixed[:channels * bands].reshape(channels, bands, -1)
    back_im = mixed[channels * bands:].reshape(channels, bands, -1)
    return (lax.optimization_barrier(jnp.sum(form[:, None, :] * back_re, 0)), lax.optimization_barrier(jnp.sum(form[:, None, :] * back_im, 0)))

def subtract_span(image_re, image_im, flat_re, flat_im, coef_re, coef_im):
    span_re = contract(coef_re, flat_re, 0, 0) - contract(coef_im, flat_im, 0, 0)
    span_im = contract(coef_re, flat_im, 0, 0) + contract(coef_im, flat_re, 0, 0)
    return (image_re - span_re, image_im - span_im)

def combine_rows(solved_re, solved_im, wave_re, wave_im):
    out_re = contract(solved_re, wave_re, 0, 0) - contract(solved_im, wave_im, 0, 0)
    out_im = contract(solved_re, wave_im, 0, 0) + contract(solved_im, wave_re, 0, 0)
    return (out_re, out_im)

def cholesky_upper(gram_re, gram_im):
    size = gram_re.shape[0]
    ticks = jnp.arange(size)

    def one_row(row_index, carry):
        upper_re, upper_im = carry
        column_re = upper_re[:, row_index]
        column_im = upper_im[:, row_index]
        total_re = gram_re[row_index] - (jnp.dot(column_re, upper_re, precision=exact_mode) + jnp.dot(column_im, upper_im, precision=exact_mode))
        total_im = gram_im[row_index] - (jnp.dot(column_re, upper_im, precision=exact_mode) - jnp.dot(column_im, upper_re, precision=exact_mode))
        pivot = jnp.sqrt(total_re[row_index])
        new_re = jnp.where(ticks >= row_index, total_re / pivot, 0.0)
        new_im = jnp.where(ticks > row_index, total_im / pivot, 0.0)
        return (upper_re.at[row_index].set(new_re), upper_im.at[row_index].set(new_im))
    zero = jnp.zeros((size, size), gram_re.dtype)
    return lax.fori_loop(0, size, one_row, (zero, zero))

def invert_upper(upper_re, upper_im):
    size = upper_re.shape[0]
    identity = jnp.eye(size, dtype=upper_re.dtype)

    def one_row(step_index, carry):
        solved_re, solved_im = carry
        row_index = size - 1 - step_index
        lead_re = upper_re[row_index]
        lead_im = upper_im[row_index]
        right_re = identity[row_index] - (jnp.dot(lead_re, solved_re, precision=exact_mode) - jnp.dot(lead_im, solved_im, precision=exact_mode))
        right_im = -(jnp.dot(lead_re, solved_im, precision=exact_mode) + jnp.dot(lead_im, solved_re, precision=exact_mode))
        pivot = upper_re[row_index, row_index]
        return (solved_re.at[row_index].set(right_re / pivot), solved_im.at[row_index].set(right_im / pivot))
    zero = jnp.zeros((size, size), upper_re.dtype)
    return lax.fori_loop(0, size, one_row, (zero, zero))

def reference(basis_re, basis_im, potential, kinetic, form_factors, channel_strength, sphere_map, column_map, atom_sites):
    block_of = jnp.arange(PW_SUB, dtype=jnp.int32) // ROWS_DEV
    depth = (sphere_map // COL_DEV).reshape(-1)
    column = (block_of[None, :] * COL_DEV + sphere_map % COL_DEV).reshape(-1)
    plane_pos = column_map[column]
    x_index = plane_pos // GRID
    y_index = plane_pos % GRID
    flat = (depth * GRID + x_index) * GRID + y_index
    psi_re = basis_re[BLOCKS - 1].reshape(SLAB, -1)
    psi_im = basis_im[BLOCKS - 1].reshape(SLAB, -1)

    def local_one(pair):
        wave_re, wave_im = pair
        empty = jnp.zeros((GRID * GRID * GRID,), jnp.float32)
        field = lax.complex(empty.at[flat].set(wave_re), empty.at[flat].set(wave_im)).reshape(GRID, GRID, GRID)
        spread = jnp.fft.ifftn(field)
        back = jnp.fft.fftn(potential * spread).reshape(-1)[flat]
        return (jnp.real(back), jnp.imag(back))
    local_re, local_im = lax.map(local_one, (psi_re, psi_im))
    form_flat = form_factors.reshape(CHANNELS, -1)
    weighted = weigh(form_flat, psi_re, psi_im)
    root_waves = math.sqrt(PWAVES)
    site_blocks = atom_sites.reshape(3, ATOMS // 64, 64).transpose(1, 0, 2)

    def one_block(carry, sites):
        phase = phase_table(depth, x_index, y_index, sites, GRID)
        sum_re, sum_im = project(weighted, phase)
        back_re, back_im = apply_back(form_flat, sum_re, sum_im, channel_strength, phase, root_waves)
        return ((carry[0] + back_re, carry[1] + back_im), None)
    zero = jnp.zeros((SLAB, PWAVES), jnp.float32)
    (near_re, near_im), unused = lax.scan(one_block, (zero, zero), site_blocks)
    kinetic_flat = kinetic.reshape(-1)
    image_re = kinetic_flat * psi_re + local_re + near_re
    image_im = kinetic_flat * psi_im + local_im + near_im
    flat_re = basis_re.reshape(BLOCKS * SLAB, -1)
    flat_im = basis_im.reshape(BLOCKS * SLAB, -1)
    coef_re, coef_im = conj_product(flat_re, flat_im, image_re, image_im, 1, 1.0 / PWAVES)
    res_re, res_im = subtract_span(image_re, image_im, flat_re, flat_im, coef_re, coef_im)
    gram_re, gram_im = conj_product(res_re, res_im, res_re, res_im, 1, 1.0 / PWAVES)
    upper_re, upper_im = cholesky_upper(gram_re, gram_im)
    solved_re, solved_im = invert_upper(upper_re, upper_im)
    next_re, next_im = combine_rows(solved_re, solved_im, res_re, res_im)
    return (next_re.reshape(SLAB, N_BAND, PW_SUB), next_im.reshape(SLAB, N_BAND, PW_SUB), coef_re.reshape(BLOCKS, SLAB, SLAB), coef_im.reshape(BLOCKS, SLAB, SLAB), upper_re, upper_im)
```

```python
import math

import jax
import jax.numpy as jnp
import numpy as np
from jax import lax
from jax.experimental import pallas as pl
from jax.experimental.pallas import tpu as pltpu
from jax.sharding import PartitionSpec as P

f32 = jnp.float32
bf16 = jnp.bfloat16
exact_mode = lax.Precision.HIGHEST

COS_POLY = (0.9999999403953552, -4.934792995452881, 4.058411121368408, -1.331876516342163, 0.21968960762023926)
SIN_POLY = (3.1415927410125732, -5.167710304260254, 2.550077438354492, -0.598291277885437, 0.07765766233205795)


def dot(left, right, left_dim=1, right_dim=0, precision=None):
    return lax.dot_general(
        left,
        right,
        (((left_dim,), (right_dim,)), ((), ())),
        precision=precision,
        preferred_element_type=f32,
    )


def split(part):
    high = part.astype(bf16)
    return high, (part - high.astype(f32)).astype(bf16)


def dot3(left, right, left_dim=1, right_dim=0):
    lh, ll = left
    rh, rl = right
    return (
        dot(lh, rh, left_dim, right_dim)
        + dot(ll, rh, left_dim, right_dim)
        + dot(lh, rl, left_dim, right_dim)
    )


def transform_tables(grid, planes):
    cos = np.array([math.cos(2.0 * math.pi * t / grid) for t in range(grid)])
    sin = np.array([math.sin(2.0 * math.pi * t / grid) for t in range(grid)])
    ticks = np.arange(grid)
    turns = ticks[:, None] * ticks[None, :] % grid
    order = ticks.reshape(grid // planes, planes).T.reshape(-1)

    def pieces(table):
        table = table.astype(np.float32)
        high = table.astype(jnp.bfloat16)
        low = (table - high.astype(np.float32)).astype(jnp.bfloat16)
        return [high, low]

    flat = np.stack(pieces(cos[turns]) + pieces(sin[turns]))
    by_owner = np.stack(pieces(cos[turns[order]]) + pieces(sin[turns[order]]))
    return flat, by_owner


def stripes(part, count):
    rows = part.shape[0] // count
    return jnp.concatenate([part[i * rows : (i + 1) * rows] for i in range(count)], 1)


def unstripe(part, count):
    width = part.shape[1] // count
    return jnp.concatenate([part[:, i * width : (i + 1) * width] for i in range(count)], 0)


def kernel_call(kernel, outs, *args, flops=10**6, vmem=32):
    return pl.pallas_call(
        kernel,
        out_shape=outs,
        in_specs=[pl.BlockSpec(memory_space=pltpu.VMEM)] * len(args),
        out_specs=jax.tree.map(lambda _: pl.BlockSpec(memory_space=pltpu.VMEM), outs),
        compiler_params=pltpu.CompilerParams(vmem_limit_bytes=vmem * 2**20),
        cost_estimate=pl.CostEstimate(flops=flops, bytes_accessed=4 * 10**6, transcendentals=0),
    )(*args)


def shape(*dims, dtype=f32):
    return jax.ShapeDtypeStruct(dims, dtype)


def pack_kernel(re_ref, im_ref, basis_ref, send_ref):
    rows = re_ref.shape[0] // 2
    bands = send_ref.shape[0]

    def whole(ref):
        return jnp.concatenate(
            [ref[pl.ds(0, rows, stride=2), :], ref[pl.ds(1, rows, stride=2), :]], 1
        )

    basis = jnp.concatenate([whole(re_ref), whole(im_ref)], 0)
    basis_ref[...] = basis
    mixed = dot(basis, basis, 1, 1, exact_mode)
    over_re = mixed[:rows, :rows] + mixed[rows:, rows:]
    over_im = mixed[:rows, rows:] - mixed[rows:, :rows]
    line = lax.broadcasted_iota(jnp.int32, (rows, rows), 0)
    spot = lax.broadcasted_iota(jnp.int32, (rows, rows), 1)
    packed = stripes(jnp.where(line <= spot, over_re, over_im), 2)
    first = 2 * (rows - bands)
    for band in range(bands):
        send_ref[band, 0:2, :] = re_ref[first + 2 * band : first + 2 * band + 2, :]
        send_ref[band, 2:4, :] = im_ref[first + 2 * band : first + 2 * band + 2, :]
        send_ref[band, 4:8, :] = packed[4 * band : 4 * band + 4, :]


def phase_kernel(grid, columns, map_ref, place_ref, sites_ref, phase_ref):
    atoms = sites_ref.shape[0]
    groups, rows = map_ref.shape
    sites = sites_ref[...].astype(bf16)
    column_x = place_ref[:, 0:1].astype(f32)
    column_y = place_ref[:, 1:2].astype(f32)
    ticks = lax.broadcasted_iota(jnp.int32, (columns, rows), 0)
    for s in range(groups):
        cell = map_ref[s : s + 1, :]
        depth = lax.div(cell, columns).astype(f32)
        hot = ticks == lax.rem(cell, columns)
        x = jnp.sum(jnp.where(hot, column_x, 0.0), 0, keepdims=True)
        y = jnp.sum(jnp.where(hot, column_y, 0.0), 0, keepdims=True)
        place = jnp.concatenate([depth, x, y, jnp.zeros((5, rows), f32)], 0).astype(bf16)
        turns = dot(sites, place)
        turns = turns - grid * jnp.floor(turns * (1.0 / grid) + 0.5)
        u = turns * (1.0 / grid)
        w = u * u
        c = COS_POLY[4]
        for k in (3, 2, 1, 0):
            c = c * w + COS_POLY[k]
        h = SIN_POLY[4]
        for k in (3, 2, 1, 0):
            h = h * w + SIN_POLY[k]
        h = h * u
        twice = h + h
        phase_ref[0:atoms, s * rows : (s + 1) * rows] = (1.0 - twice * h).astype(bf16)
        phase_ref[atoms : 2 * atoms, s * rows : (s + 1) * rows] = (twice * c).astype(bf16)


def two_rows(ref, s, line):
    return jnp.concatenate([ref[s, line : line + 1, :], ref[s, line + 1 : line + 2, :]], 1)


def columns_kernel(columns, map_ref, form_ref, phase_ref, table_ref, got_ref, send_ref):
    groups, rows = map_ref.shape
    atoms = phase_ref.shape[0] // 2
    grid = table_ref.shape[1]
    planes = send_ref.shape[1]
    owners = send_ref.shape[0]
    channels = form_ref.shape[0]
    ticks = lax.broadcasted_iota(jnp.int32, (columns, rows), 0)
    deep = lax.broadcasted_iota(jnp.int32, (grid, rows), 0)
    total = jnp.zeros((4 * columns, grid), f32)
    first, second = [], []
    for s in range(groups):
        psi_re = two_rows(got_ref, s, 0)
        psi_im = two_rows(got_ref, s, 2)
        cell = map_ref[s : s + 1, :]
        depth_hot = (deep == lax.div(cell, columns)).astype(f32).astype(bf16)
        hot = ticks == lax.rem(cell, columns)
        spread = jnp.concatenate([jnp.where(hot, psi_re, 0.0), jnp.where(hot, psi_im, 0.0)], 0)
        total = total + dot(jnp.concatenate(split(spread), 0), depth_hot, 1, 1)
        form = form_ref[:, s, :]
        weighted_re = (form * psi_re).astype(bf16)
        weighted_im = (form * psi_im).astype(bf16)
        first.append(jnp.concatenate([weighted_re, weighted_im], 0))
        second.append(jnp.concatenate([-weighted_im, weighted_re], 0))
    column = split(total[: 2 * columns] + total[2 * columns :])
    by_cos = dot3((table_ref[0], table_ref[1]), column, 1, 1)
    by_sin = dot3((table_ref[2], table_ref[3]), column, 1, 1)
    deep_re = by_cos[:, :columns] - by_sin[:, columns:]
    deep_im = by_sin[:, :columns] + by_cos[:, columns:]
    products = dot(phase_ref[0:atoms, :], jnp.concatenate(first, 1), 1, 1) + dot(
        phase_ref[atoms : 2 * atoms, :], jnp.concatenate(second, 1), 1, 1
    )
    parts = [products[owners * k : owners * (k + 1)] for k in range(atoms // owners)]
    half = len(parts) // 2
    overlap = jnp.sum(got_ref[:, 4:8, :], 0).T
    own = jnp.concatenate(
        [overlap[:owners], overlap[owners:], jnp.zeros((owners, 2 * columns - 8), f32)], 1
    )
    extra = [
        jnp.concatenate(parts[:half], 1),
        jnp.concatenate(parts[half:], 1),
        own,
    ]
    for k in range(planes):
        lines = slice(owners * k, owners * (k + 1))
        send_ref[:, k, :] = jnp.concatenate([deep_re[lines], deep_im[lines], extra[k]], 1)


def planes_kernel(columns, place_ref, pot_ref, table_ref, got_ref, send_ref):
    planes, grid, _ = pot_ref.shape
    owners = got_ref.shape[0]
    steps, lanes = place_ref.shape[1:]
    packs = lanes // owners
    ticks = lax.broadcasted_iota(jnp.int32, (grid, lanes), 0)
    cos = (table_ref[0], table_ref[1])
    sin = (table_ref[2], table_ref[3])
    values = []
    for k in range(planes):
        turned = got_ref[:, k, :].T
        for part in range(2):
            high, low = split(stripes(turned[part * columns : (part + 1) * columns], packs))
            values.append((high.astype(f32), low.astype(f32)))
    field = jnp.zeros((2 * planes * grid, grid), f32)
    hots = []
    for q in range(steps):
        hot_x = ticks == place_ref[0, q : q + 1, :]
        hot_y = (ticks == place_ref[1, q : q + 1, :]).astype(f32).astype(bf16)
        hots.append((hot_x, hot_y))
        for piece in range(2):
            spread = jnp.concatenate(
                [jnp.where(hot_x, v[piece][q : q + 1, :], 0.0).astype(bf16) for v in values], 0
            )
            field = field + dot(spread, hot_y, 1, 1)

    def along_y(parts):
        pieces = split(jnp.concatenate(parts, 0))
        return dot3(pieces, cos), dot3(pieces, sin)

    parts = [field[i * grid : (i + 1) * grid] for i in range(2 * planes)]
    by_cos, by_sin = along_y(parts)
    back = []
    for k in range(planes):
        re = slice(2 * k * grid, (2 * k + 1) * grid)
        im = slice((2 * k + 1) * grid, (2 * k + 2) * grid)
        now_re = split(by_cos[re] - by_sin[im])
        now_im = split(by_sin[re] + by_cos[im])
        real = dot3(cos, now_re) - dot3(sin, now_im)
        imag = dot3(sin, now_re) + dot3(cos, now_im)
        scaled = pot_ref[k] * (1.0 / grid**3)
        real = split(real * scaled)
        imag = split(imag * scaled)
        back.append(dot3(cos, real) + dot3(sin, imag))
        back.append(dot3(cos, imag) - dot3(sin, real))
    by_cos, by_sin = along_y(back)
    final = []
    for k in range(planes):
        re = slice(2 * k * grid, (2 * k + 1) * grid)
        im = slice((2 * k + 1) * grid, (2 * k + 2) * grid)
        final.append(by_cos[re] + by_sin[im])
        final.append(by_cos[im] - by_sin[re])
    high, low = split(jnp.concatenate(final, 0))
    found = [[] for _ in final]
    for q in range(steps):
        hot_x, hot_y = hots[q]
        mixed = dot(high, hot_y) + dot(low, hot_y)
        for i in range(2 * planes):
            picked = jnp.where(hot_x, mixed[i * grid : (i + 1) * grid], 0.0)
            found[i].append(jnp.sum(picked, 0, keepdims=True))
    for k in range(planes):
        halves = [unstripe(jnp.concatenate(found[2 * k + i], 0), packs) for i in range(2)]
        turned = jnp.concatenate(halves, 0).T
        ride = jnp.sum(got_ref[:, k, 2 * columns :], 0, keepdims=True)
        send_ref[:, k, :] = jnp.concatenate(
            [turned, jnp.broadcast_to(ride, (owners, ride.shape[1]))], 1
        )


def image_kernel(
    columns, waves, map_ref, form_ref, kinetic_ref, strength_ref, phase_ref, table_ref, psi_ref, got_ref, send_ref
):
    groups, rows = map_ref.shape
    atoms = phase_ref.shape[0] // 2
    grid = table_ref.shape[1]
    owners, planes, _ = got_ref.shape
    channels = form_ref.shape[0]
    root = math.sqrt(waves)
    got = [got_ref[:, k, :] for k in range(planes)]
    ride = [g[:, 2 * columns :] for g in got]
    wide = 2 * channels
    per_row = 2 * columns // wide
    sums = jnp.concatenate(
        [r[:, wide * i : wide * (i + 1)] for r in ride[:2] for i in range(per_row)], 0
    ).T
    factor = jnp.concatenate([strength_ref[...], strength_ref[...]], 0)
    scaled = factor * (sums / root) / root
    scaled_re = scaled[:channels].astype(bf16)
    scaled_im = scaled[channels:].astype(bf16)
    mixed = dot(jnp.concatenate([scaled_re, scaled_im], 0), phase_ref[0:atoms, :]) + dot(
        jnp.concatenate([scaled_im, -scaled_re], 0), phase_ref[atoms : 2 * atoms, :]
    )
    deep = split(jnp.concatenate([g[:, : 2 * columns] for g in got], 0).T)
    by_cos = dot3(deep, (table_ref[0], table_ref[1]))
    by_sin = dot3(deep, (table_ref[2], table_ref[3]))
    out_re = by_cos[:columns] + by_sin[columns:]
    out_im = by_cos[columns:] - by_sin[:columns]
    out = jnp.concatenate(split(jnp.concatenate([out_re, out_im], 0)), 0)
    ticks = lax.broadcasted_iota(jnp.int32, (columns, rows), 0)
    depths = lax.broadcasted_iota(jnp.int32, (grid, rows), 0)
    overlap = jnp.concatenate([ride[2][:, 0:4].T, ride[2][:, 4:8].T], 1)
    for s in range(groups):
        cell = map_ref[s : s + 1, :]
        depth_hot = (depths == lax.div(cell, columns)).astype(f32).astype(bf16)
        hot = ticks == lax.rem(cell, columns)
        found = dot(out, depth_hot)
        found = found[: 2 * columns] + found[2 * columns :]
        local_re = jnp.sum(jnp.where(hot, found[:columns], 0.0), 0, keepdims=True)
        local_im = jnp.sum(jnp.where(hot, found[columns:], 0.0), 0, keepdims=True)
        form = form_ref[:, s, :]
        lanes = slice(s * rows, (s + 1) * rows)
        near_re = jnp.sum(form * mixed[:channels, lanes], 0, keepdims=True)
        near_im = jnp.sum(form * mixed[channels:, lanes], 0, keepdims=True)
        kinetic = kinetic_ref[s : s + 1, :]
        image_re = kinetic * two_rows(psi_ref, s, 0) + local_re + near_re
        image_im = kinetic * two_rows(psi_ref, s, 2) + local_im + near_im
        send_ref[s, 0:1, :] = image_re[:, :128]
        send_ref[s, 1:2, :] = image_re[:, 128:]
        send_ref[s, 2:3, :] = image_im[:, :128]
        send_ref[s, 3:4, :] = image_im[:, 128:]
        send_ref[s, 4:8, :] = overlap


def products_kernel(waves, basis_ref, got_ref, image_ref, send_ref):
    bands = got_ref.shape[0]
    half = basis_ref.shape[0] // 2
    owners = send_ref.shape[0]
    image_re = jnp.concatenate([got_ref[:, 0, :], got_ref[:, 1, :]], 1)
    image_im = jnp.concatenate([got_ref[:, 2, :], got_ref[:, 3, :]], 1)
    image = jnp.concatenate([image_re, image_im], 0)
    image_ref[...] = image
    mixed = dot(image, basis_ref[...], 1, 1, exact_mode) * (1.0 / waves)
    coef_re = mixed[:bands, :half] + mixed[bands:, half:]
    coef_im = mixed[bands:, :half] - mixed[:bands, half:]
    coef = jnp.concatenate([coef_re, coef_im], 1)
    own = dot(image, image, 1, 1, exact_mode) * (1.0 / waves)
    own_re = own[:bands, :bands] + own[bands:, bands:]
    own_im = own[:bands, bands:] - own[bands:, :bands]
    line = lax.broadcasted_iota(jnp.int32, (bands, bands), 0)
    spot = lax.broadcasted_iota(jnp.int32, (bands, bands), 1)
    packed = jnp.where(line <= spot, own_re, own_im)
    row = jnp.concatenate(
        [stripes(coef, bands), stripes(packed, bands), jnp.zeros((1, 128 - bands * bands), f32)], 1
    )
    send_ref[:, 0, :] = jnp.broadcast_to(row, (owners, row.shape[1]))


def overlap_kernel(waves, got_ref, over_ref):
    size = over_ref.shape[0] // 2
    packed = jnp.concatenate([got_ref[d, 4:8, :] for d in range(got_ref.shape[0])], 0)
    packed = unstripe(packed, 2) * (1.0 / waves)
    line = lax.broadcasted_iota(jnp.int32, (size, size), 0)
    spot = lax.broadcasted_iota(jnp.int32, (size, size), 1)
    turned = packed.T
    over_re = jnp.where(line <= spot, packed, turned)
    over_im = jnp.where(line < spot, -turned, jnp.where(line > spot, packed, 0.0))
    over_ref[...] = jnp.concatenate(
        [jnp.concatenate([over_re, -over_im], 1), jnp.concatenate([over_im, over_re], 1)], 0
    )


def gather_kernel(got_ref, send_ref):
    row = jnp.sum(got_ref[:, 0, :], 0, keepdims=True)
    send_ref[:, 0, :] = jnp.broadcast_to(row, (send_ref.shape[0], row.shape[1]))


def finish_kernel(
    basis_ref, image_ref, over_ref, got_ref, next_re_ref, next_im_ref, coef_re_ref, coef_im_ref, chol_re_ref, chol_im_ref
):
    bands = image_ref.shape[0] // 2
    half = basis_ref.shape[0] // 2
    row = jnp.sum(got_ref[:, 0, :], 0, keepdims=True)
    size = bands * 2 * half
    coef = unstripe(row[:, :size], bands)
    packed = unstripe(row[:, size : size + bands * bands], bands)
    coef_re = coef[:, :half]
    coef_im = coef[:, half:]
    coef_re_ref[...] = coef_re.T
    coef_im_ref[...] = coef_im.T
    line = lax.broadcasted_iota(jnp.int32, (bands, bands), 0)
    spot = lax.broadcasted_iota(jnp.int32, (bands, bands), 1)
    turned = packed.T
    own_re = jnp.where(line <= spot, packed, turned)
    own_im = jnp.where(line < spot, -turned, jnp.where(line > spot, packed, 0.0))
    left = dot(coef, over_ref[...], 1, 0, exact_mode) - 2.0 * coef
    stacked = jnp.concatenate([coef, jnp.concatenate([-coef_im, coef_re], 1)], 0)
    mixed = dot(stacked, left, 1, 1, exact_mode)
    gram_re = own_re + mixed[:bands]
    gram_im = own_im + mixed[bands:]
    eye = jnp.where(line == spot, 1.0, 0.0)
    work_re = jnp.concatenate([gram_re, eye], 1)
    work_im = jnp.concatenate([gram_im, jnp.zeros_like(eye)], 1)
    rows_re, rows_im = [], []
    for k in range(bands):
        pivot = lax.rsqrt(work_re[k : k + 1, k : k + 1])
        lead_re = work_re[k : k + 1, :] * pivot
        lead_im = work_im[k : k + 1, :] * pivot
        rows_re.append(lead_re)
        rows_im.append(lead_im)
        if k + 1 < bands:
            column_re = work_re[:, k : k + 1] * pivot
            column_im = work_im[:, k : k + 1] * pivot
            work_re, work_im = (
                work_re - (column_re * lead_re - column_im * lead_im),
                work_im - (column_re * lead_im + column_im * lead_re),
            )
    all_re = jnp.concatenate(rows_re, 0)
    all_im = jnp.concatenate(rows_im, 0)
    chol_re_ref[...] = jnp.where(line <= spot, all_re[:, :bands], 0.0)
    chol_im_ref[...] = jnp.where(line < spot, all_im[:, :bands], 0.0)
    inv_re = all_re[:, bands:]
    inv_im = all_im[:, bands:]
    basis_re = basis_ref[0:half, :]
    basis_im = basis_ref[half : 2 * half, :]
    span_re = dot(coef, jnp.concatenate([basis_re, -basis_im], 0), 1, 0, exact_mode)
    span_im = dot(coef, jnp.concatenate([basis_im, basis_re], 0), 1, 0, exact_mode)
    rest_re = image_ref[0:bands, :] - span_re
    rest_im = image_ref[bands : 2 * bands, :] - span_im
    next_re = dot(inv_re, rest_re, 1, 0, exact_mode) + dot(inv_im, rest_im, 1, 0, exact_mode)
    next_im = dot(inv_re, rest_im, 1, 0, exact_mode) - dot(inv_im, rest_re, 1, 0, exact_mode)
    for ref, value in ((next_re_ref, next_re), (next_im_ref, next_im)):
        ref[pl.ds(0, bands, stride=2), :] = value[:, :128]
        ref[pl.ds(1, bands, stride=2), :] = value[:, 128:]


def body(
    basis_re,
    basis_im,
    potential,
    kinetic,
    form_factors,
    channel_strength,
    sphere_map,
    column_map,
    atom_sites,
):
    blocks, slab, _, row_count = basis_re.shape
    band_count = lax.axis_size("band")
    owners = lax.axis_size("pw")
    planes, grid, _ = potential.shape
    columns = column_map.shape[0] // owners
    waves = band_count * owners * row_count
    atoms = atom_sites.shape[1]
    rows = blocks * slab
    flat_table, owner_table = transform_tables(grid, planes)
    flat_table = jnp.asarray(flat_table)
    owner_table = jnp.asarray(owner_table)

    def exchange(part, axis):
        return lax.all_to_all(part, axis, split_axis=0, concat_axis=0, tiled=True)

    basis, send = kernel_call(
        pack_kernel,
        (shape(2 * rows, row_count), shape(slab, 8, 128)),
        basis_re.reshape(-1, 128),
        basis_im.reshape(-1, 128),
    )
    psi = exchange(send, "band")

    x_index = column_map // grid
    y_index = column_map % grid
    both = jnp.stack([x_index, y_index])
    mine = lax.dynamic_slice_in_dim(both, lax.axis_index("pw") * columns, columns, 1).T
    spread = both.reshape(2, owners, columns // 8, 8).transpose(0, 3, 2, 1).reshape(2, 8, -1)
    sites = jnp.pad(atom_sites, ((0, 5), (0, 0))).T.astype(f32)
    phase = kernel_call(
        lambda *refs: phase_kernel(grid, columns, *refs),
        shape(2 * atoms, band_count * row_count, dtype=bf16),
        sphere_map,
        mine,
        sites,
        flops=10**7,
    )
    send = kernel_call(
        lambda *refs: columns_kernel(columns, *refs),
        shape(owners, planes, 128),
        sphere_map,
        form_factors,
        phase,
        owner_table,
        psi,
    )
    got = exchange(send, "pw")
    send = kernel_call(
        lambda *refs: planes_kernel(columns, *refs),
        shape(owners, planes, 128),
        spread,
        potential,
        flat_table,
        got,
        vmem=48,
    )
    got = exchange(send, "pw")
    send = kernel_call(
        lambda *refs: image_kernel(columns, waves, *refs),
        shape(band_count, 8, 128),
        sphere_map,
        form_factors,
        kinetic,
        channel_strength[:, None],
        phase,
        owner_table,
        psi,
        got,
    )
    got = exchange(send, "band")
    image, send = kernel_call(
        lambda *refs: products_kernel(waves, *refs),
        (shape(2 * slab, row_count), shape(owners, 1, 9 * 128)),
        basis,
        got,
    )
    over = kernel_call(
        lambda *refs: overlap_kernel(waves, *refs), shape(2 * rows, 2 * rows), got
    )
    got = exchange(send, "pw")
    send = kernel_call(gather_kernel, shape(band_count, 1, 9 * 128), got)
    got = exchange(send, "band")
    next_re, next_im, coef_re, coef_im, chol_re, chol_im = kernel_call(
        finish_kernel,
        (
            shape(2 * slab, 128),
            shape(2 * slab, 128),
            shape(rows, slab),
            shape(rows, slab),
            shape(slab, slab),
            shape(slab, slab),
        ),
        basis,
        image,
        over,
        got,
    )
    return (
        next_re.reshape(slab, 1, row_count),
        next_im.reshape(slab, 1, row_count),
        coef_re.reshape(blocks, slab, slab),
        coef_im.reshape(blocks, slab, slab),
        chol_re,
        chol_im,
    )


def solution(mesh):
    return jax.shard_map(
        body,
        mesh=mesh,
        in_specs=(
            P(None, None, "band", "pw"),
            P(None, None, "band", "pw"),
            P("pw", None, None),
            P(None, "pw"),
            P(None, None, "pw"),
            P(),
            P(None, "pw"),
            P(),
            P(),
        ),
        out_specs=(P(None, "band", "pw"), P(None, "band", "pw"), P(), P(), P(), P()),
        check_vma=False,
    )
```

```python
import math

import jax
import jax.numpy as jnp
import numpy as np
from jax import lax
from jax.experimental import pallas as pl
from jax.experimental.pallas import tpu as pltpu
from jax.sharding import PartitionSpec as P

f32 = jnp.float32
bf16 = jnp.bfloat16
exact_mode = lax.Precision.HIGHEST

COS_POLY = (0.9999999403953552, -4.934792995452881, 4.058411121368408, -1.331876516342163, 0.21968960762023926)
SIN_POLY = (3.1415927410125732, -5.167710304260254, 2.550077438354492, -0.598291277885437, 0.07765766233205795)


def dot(left, right, left_dim=1, right_dim=0, precision=None):
    return lax.dot_general(
        left,
        right,
        (((left_dim,), (right_dim,)), ((), ())),
        precision=precision,
        preferred_element_type=f32,
    )


def split(part):
    high = part.astype(bf16)
    return high, (part - high.astype(f32)).astype(bf16)


def split3(part):
    high = part.astype(bf16)
    rest = part - high.astype(f32)
    middle = rest.astype(bf16)
    return [high, middle, (rest - middle.astype(f32)).astype(bf16)]


def dot3(left, right, left_dim=1, right_dim=0):
    lh, ll = left
    rh, rl = right
    return (
        dot(lh, rh, left_dim, right_dim)
        + dot(ll, rh, left_dim, right_dim)
        + dot(lh, rl, left_dim, right_dim)
    )


def pieces(table):
    table = table.astype(np.float32)
    high = table.astype(jnp.bfloat16)
    return [high, (table - high.astype(np.float32)).astype(jnp.bfloat16)]


def transform_tables(grid, planes, half_x, half_y):
    cos = np.array([math.cos(2.0 * math.pi * t / grid) for t in range(grid)])
    sin = np.array([math.sin(2.0 * math.pi * t / grid) for t in range(grid)])
    ticks = np.arange(grid)
    turns = ticks[:, None] * ticks[None, :] % grid
    order = ticks.reshape(grid // planes, planes).T.reshape(-1)
    by_owner = np.stack(pieces(cos[turns[order]]) + pieces(sin[turns[order]]))
    top = grid // 2 + 1

    def folded(half):
        table = np.zeros((2 * half, 2 * half))
        table[:top, :top] = cos[turns[:top, :top]]
        table[half + 1 : half + top - 1, half + 1 : half + top - 1] = sin[
            turns[1 : top - 1, 1 : top - 1]
        ]
        return pieces(table)

    high, low = folded(half_x)
    table_x = np.concatenate([high, low, high], 1)
    high, low = folded(half_y)
    table_y = np.concatenate([high, high, low], 0)
    return by_owner, table_x, table_y


def stripes(part, count):
    rows = part.shape[0] // count
    return jnp.concatenate([part[i * rows : (i + 1) * rows] for i in range(count)], 1)


def unstripe(part, count):
    width = part.shape[1] // count
    return jnp.concatenate([part[:, i * width : (i + 1) * width] for i in range(count)], 0)


def kernel_call(kernel, outs, *args, flops=10**6, vmem=8, scratch=(), far=(), far_out=(), grid=()):
    single = not isinstance(outs, tuple)
    outs = (outs,) if single else outs
    place = (pl.BlockSpec(memory_space=pltpu.VMEM), pl.BlockSpec(memory_space=pltpu.HBM))
    out = pl.pallas_call(
        kernel,
        out_shape=outs,
        in_specs=[place[i in far] for i in range(len(args))],
        scratch_shapes=scratch,
        grid=grid,
        out_specs=tuple(place[i in far_out] for i in range(len(outs))),
        compiler_params=pltpu.CompilerParams(vmem_limit_bytes=vmem * 2**20),
        cost_estimate=pl.CostEstimate(flops=flops, bytes_accessed=4 * 10**6, transcendentals=0),
    )(*args)
    return out[0] if single else out


def shape(*dims, dtype=f32):
    return jax.ShapeDtypeStruct(dims, dtype)


def pack_kernel(
    far_re_ref,
    far_im_ref,
    far_map_ref,
    far_place_ref,
    far_sites_ref,
    basis_ref,
    send_ref,
    small_ref,
    re_ref,
    im_ref,
    map_ref,
    place_ref,
    sites_ref,
    sems,
    small_sems,
):
    count = sems.shape[1]
    small = [
        pltpu.make_async_copy(far, near, small_sems.at[i])
        for i, (far, near) in enumerate(
            ((far_map_ref, map_ref), (far_place_ref, place_ref), (far_sites_ref, sites_ref))
        )
    ]
    size = re_ref.shape[0] // count
    copies = [
        pltpu.make_async_copy(
            far.at[pl.ds(i * size, size)], near.at[pl.ds(i * size, size)], sems.at[part, i]
        )
        for part, (far, near) in enumerate(((far_re_ref, re_ref), (far_im_ref, im_ref)))
        for i in range(count)
    ]
    for copy in copies + small:
        copy.start()
    for copy in copies + small:
        copy.wait()
    count = map_ref.shape[0]
    lines = place_ref.shape[0] // 2
    small_ref[0:count, :] = map_ref[...]
    small_ref[count : count + lines, :] = jnp.concatenate(
        [place_ref[0:lines, :], place_ref[lines:, :]], 1
    )
    small_ref[count + lines :, :] = jnp.concatenate(
        [
            sites_ref[:, 0 : small_ref.shape[1]],
            sites_ref[:, small_ref.shape[1] :],
            jnp.zeros((2, small_ref.shape[1]), jnp.int32),
        ],
        0,
    )
    rows = re_ref.shape[0] // 2
    bands = send_ref.shape[0]

    def whole(ref):
        return jnp.concatenate(
            [ref[pl.ds(0, rows, stride=2), :], ref[pl.ds(1, rows, stride=2), :]], 1
        )

    basis = jnp.concatenate([whole(re_ref), whole(im_ref)], 0)
    basis_ref[...] = basis
    mixed = dot(basis, basis, 1, 1, exact_mode)
    over_re = mixed[:rows, :rows] + mixed[rows:, rows:]
    over_im = mixed[:rows, rows:] - mixed[rows:, :rows]
    line = lax.broadcasted_iota(jnp.int32, (rows, rows), 0)
    spot = lax.broadcasted_iota(jnp.int32, (rows, rows), 1)
    packed = stripes(jnp.where(line <= spot, over_re, over_im), 2)
    first = 2 * (rows - bands)
    for band in range(bands):
        send_ref[band, 0:2, :] = re_ref[first + 2 * band : first + 2 * band + 2, :]
        send_ref[band, 2:4, :] = im_ref[first + 2 * band : first + 2 * band + 2, :]
        send_ref[band, 4:8, :] = packed[4 * band : 4 * band + 4, :]


def phase_kernel(grid, columns, small_ref, far_ref, phase_ref, sems):
    groups, _, rows = phase_ref.shape
    atoms = phase_ref.shape[1] // 2
    sites = jnp.concatenate([small_ref[16:19, :], small_ref[19:22, :]], 1).astype(f32)
    sites = jnp.concatenate([sites, jnp.zeros((5, atoms), f32)], 0).astype(bf16)
    owner = lax.axis_index("pw")
    packs = rows // columns
    row = lax.div(owner, packs // 2)
    line = small_ref[pl.ds(groups + lax.rem(row, groups), 1), :]
    block = lax.div(row, groups) * (packs // 2) + lax.rem(owner, packs // 2)
    mine = jnp.zeros((1, columns), jnp.int32)
    for j in range(packs):
        chosen = (block == j).astype(jnp.int32)
        mine = mine + chosen * line[:, j * columns : (j + 1) * columns]
    mine = jnp.concatenate([mine, jnp.zeros((7, columns), jnp.int32)], 0).T[:, 0:1]
    column_x = lax.div(mine, grid).astype(f32)
    column_y = lax.rem(mine, grid).astype(f32)
    ticks = lax.broadcasted_iota(jnp.int32, (columns, rows), 0)
    for s in range(groups):
        cell = small_ref[s : s + 1, :]
        depth = lax.div(cell, columns).astype(f32)
        hot = ticks == lax.rem(cell, columns)
        x = jnp.sum(jnp.where(hot, column_x, 0.0), 0, keepdims=True)
        y = jnp.sum(jnp.where(hot, column_y, 0.0), 0, keepdims=True)
        place = jnp.concatenate([depth, x, y, jnp.zeros((5, rows), f32)], 0).astype(bf16)
        turns = dot(sites, place, 0, 0)
        turns = turns - grid * jnp.floor(turns * (1.0 / grid) + 0.5)
        u = turns * (1.0 / grid)
        w = u * u
        c = COS_POLY[4]
        for k in (3, 2, 1, 0):
            c = c * w + COS_POLY[k]
        h = SIN_POLY[4]
        for k in (3, 2, 1, 0):
            h = h * w + SIN_POLY[k]
        h = h * u
        twice = h + h
        phase_ref[s, 0:atoms, :] = (1.0 - twice * h).astype(bf16)
        phase_ref[s, atoms : 2 * atoms, :] = (twice * c).astype(bf16)
        pltpu.make_async_copy(phase_ref.at[s], far_ref.at[s], sems.at[s]).start()
    for s in range(groups):
        pltpu.make_async_copy(phase_ref.at[s], far_ref.at[s], sems.at[s]).wait()


def two_rows(ref, s, line):
    return jnp.concatenate([ref[s, line : line + 1, :], ref[s, line + 1 : line + 2, :]], 1)


def make_copies(far_ref, near_ref, sems):
    return [
        pltpu.make_async_copy(far_ref.at[i], near_ref.at[i], sems.at[i])
        for i in range(near_ref.shape[0])
    ]


def fetch(far_ref, near_ref, sems):
    copies = make_copies(far_ref, near_ref, sems)
    for copy in copies:
        copy.start()
    return copies


def columns_kernel(
    columns, small_ref, form_ref, far_ref, table_ref, got_ref, send_ref, phase_ref, sems
):
    copies = fetch(far_ref, phase_ref, sems)
    groups, _, rows = phase_ref.shape
    atoms = phase_ref.shape[1] // 2
    grid = table_ref.shape[1]
    planes = send_ref.shape[1]
    owners = send_ref.shape[0]
    channels = form_ref.shape[0]
    ticks = lax.broadcasted_iota(jnp.int32, (columns, rows), 0)
    deep = lax.broadcasted_iota(jnp.int32, (grid, rows), 0)
    total = jnp.zeros((4 * columns, grid), f32)
    first, second = [], []
    for s in range(groups):
        psi_re = two_rows(got_ref, s, 0)
        psi_im = two_rows(got_ref, s, 2)
        cell = small_ref[s : s + 1, :]
        depth_hot = (deep == lax.div(cell, columns)).astype(f32).astype(bf16)
        hot = ticks == lax.rem(cell, columns)
        spread = jnp.concatenate([jnp.where(hot, psi_re, 0.0), jnp.where(hot, psi_im, 0.0)], 0)
        total = total + dot(jnp.concatenate(split(spread), 0), depth_hot, 1, 1)
        form = form_ref[:, s, :]
        weighted_re = (form * psi_re).astype(bf16)
        weighted_im = (form * psi_im).astype(bf16)
        first.append(jnp.concatenate([weighted_re, weighted_im], 0))
        second.append(jnp.concatenate([-weighted_im, weighted_re], 0))
    column = split(total[: 2 * columns] + total[2 * columns :])
    by_cos = dot3((table_ref[0], table_ref[1]), column, 1, 1)
    by_sin = dot3((table_ref[2], table_ref[3]), column, 1, 1)
    deep_re = by_cos[:, :columns] - by_sin[:, columns:]
    deep_im = by_sin[:, :columns] + by_cos[:, columns:]
    products = jnp.zeros((atoms, 2 * channels), f32)
    for s in range(groups):
        copies[s].wait()
        products = products + (
            dot(phase_ref[s, 0:atoms, :], first[s], 1, 1)
            + dot(phase_ref[s, atoms : 2 * atoms, :], second[s], 1, 1)
        )
    parts = [products[owners * k : owners * (k + 1)] for k in range(atoms // owners)]
    half = len(parts) // 2
    overlap = jnp.sum(got_ref[:, 4:8, :], 0).T
    own = jnp.concatenate(
        [overlap[:owners], overlap[owners:], jnp.zeros((owners, 2 * columns - 8), f32)], 1
    )
    extra = [
        jnp.concatenate(parts[:half], 1),
        jnp.concatenate(parts[half:], 1),
        own,
    ]
    for k in range(planes):
        lines = slice(owners * k, owners * (k + 1))
        send_ref[:, k, :] = jnp.concatenate([deep_re[lines], deep_im[lines], extra[k]], 1)


def fold_kernel(pot_ref, out_ref):
    planes, grid, _ = pot_ref.shape

    def chooser(size):
        half = size // 2
        line = lax.broadcasted_iota(jnp.int32, (size, grid), 0)
        spot = lax.broadcasted_iota(jnp.int32, (size, grid), 1)
        t = jnp.where(line < half, line, line - half)
        plus = (line < half) & (t <= grid // 2) & (spot == t)
        minus = (line >= half) & (t > 0) & (t < grid // 2) & (spot == grid - t)
        return jnp.where(plus | minus, 1.0, 0.0).astype(bf16)

    lines = chooser(out_ref.shape[1])
    spots = chooser(out_ref.shape[2])
    for k in range(planes):
        part = sum(dot(lines, piece) for piece in split3(pot_ref[k]))
        part = sum(dot(piece, spots, 1, 1) for piece in split3(part))
        out_ref[k] = part * (1.0 / grid**3)


def planes_kernel(
    columns,
    grid,
    small_ref,
    fold_ref,
    table_x_ref,
    table_y_ref,
    far_ref,
    got_ref,
    send_ref,
    phase_ref,
    sems,
    value_ref,
    place_ref,
    hot_ref,
    field_ref,
):
    planes, size_x, size_y = fold_ref.shape
    half_x, half_y = size_x // 2, size_y // 2
    owners = got_ref.shape[0]
    steps, _, wide = phase_ref.shape
    lines, lanes = 2 * steps, wide // 2
    packs = lanes // columns
    ticks_x = lax.broadcasted_iota(jnp.int32, (half_x, wide), 0)
    ticks_y = lax.broadcasted_iota(jnp.int32, (half_y, wide), 0)
    count = 2 * planes

    def folded(at):
        t = jnp.minimum(at, grid - at)
        sign = jnp.where(at == t, 1.0, -1.0)
        return t.astype(f32), jnp.where((t == 0) | (2 * t == grid), 0.0, sign)

    def along_y(part):
        high, low = split(part)
        return dot(jnp.concatenate([high, low, high], 1), table_y_ref[...])

    def along_x(part):
        high, low = split(part)
        return dot(table_x_ref[...], jnp.concatenate([high, high, low], 0))

    def quarters(part):
        return (
            part[:half_x, :half_y],
            part[:half_x, half_y:],
            part[half_x:, :half_y],
            part[half_x:, half_y:],
        )

    def join(ee, eo, oe, oo):
        return jnp.concatenate(
            [jnp.concatenate([ee, eo], 1), jnp.concatenate([oe, oo], 1)], 0
        )

    step = pl.program_id(0)

    @pl.when(step == 0)
    def to_planes():
        fetch(far_ref, phase_ref, sems)
        place = small_ref[steps : 2 * steps, :]
        for i, at in enumerate((lax.div(place, grid), lax.rem(place, grid))):
            place_ref[2 * i], place_ref[2 * i + 1] = folded(at)
        for k in range(planes):
            loaded = [got_ref[pl.ds(j, lines, stride=packs), k, :] for j in range(packs)]
            for part in range(2):
                spot = slice(part * columns, (part + 1) * columns)
                value = jnp.concatenate([v[:, spot] for v in loaded], 1)
                value = jnp.concatenate([value[:steps], value[steps:]], 1)
                for piece, half in enumerate(split(value)):
                    half = half.astype(f32)
                    value_ref[piece, 2 * (2 * k + part)] = half
                    value_ref[piece, 2 * (2 * k + part) + 1] = half * place_ref[1]
        field = jnp.zeros((count * size_x, size_y), f32)
        for q in range(steps):
            hot_x = ticks_x == place_ref[0, q : q + 1, :].astype(jnp.int32)
            hot_y = ticks_y == place_ref[2, q : q + 1, :].astype(jnp.int32)
            hot_y = jnp.concatenate(
                [jnp.where(hot_y, 1.0, 0.0), jnp.where(hot_y, place_ref[3, q : q + 1, :], 0.0)], 0
            ).astype(bf16)
            hot_ref[q] = hot_y
            for piece in range(2):
                spread = [
                    jnp.where(hot_x, value_ref[piece, i, q : q + 1, :], 0.0) for i in range(2 * count)
                ]
                field = field + dot(jnp.concatenate(spread, 0).astype(bf16), hot_y, 1, 1)
        field_ref[...] = field

    @pl.when(step == 1)
    def transforms():
        field = along_y(field_ref[...])
        back = []
        for k in range(planes):
            re, im = [
                quarters(along_x(field[(2 * k + i) * size_x : (2 * k + i + 1) * size_x]))
                for i in range(2)
            ]
            values_v = quarters(fold_ref[k])
            real_sum, real_gap = re[0] - re[3], re[0] + re[3]
            imag_sum, imag_gap = im[0] - im[3], im[0] + im[3]
            cross_re, cross_re_gap = re[1] + re[2], re[1] - re[2]
            cross_im, cross_im_gap = im[1] + im[2], im[1] - im[2]
            pp_re, mm_re = real_sum - cross_im, real_sum + cross_im
            pp_im, mm_im = imag_sum + cross_re, imag_sum - cross_re
            pm_re, mp_re = real_gap + cross_im_gap, real_gap - cross_im_gap
            pm_im, mp_im = imag_gap - cross_re_gap, imag_gap + cross_re_gap
            parts = []
            for pp, pm, mp, mm in (
                (pp_re, pm_re, mp_re, mm_re),
                (pp_im, pm_im, mp_im, mm_im),
            ):
                pp, pm, mp, mm = [a * b for a, b in zip((pp, pm, mp, mm), values_v)]
                plus_s, plus_g = pp + pm, pp - pm
                minus_s, minus_g = mp + mm, mp - mm
                parts.append((plus_s + minus_s, plus_g + minus_g, plus_s - minus_s, plus_g - minus_g))
            re, im = parts
            back.append(along_x(join(re[0], im[1], im[2], -re[3])))
            back.append(along_x(join(im[0], -re[1], -re[2], -im[3])))
        field_ref[...] = along_y(jnp.concatenate(back, 0))

    @pl.when(step == 2)
    def to_columns():
        high, low = split(field_ref[...])
        for q in range(steps):
            hot_x = ticks_x == place_ref[0, q : q + 1, :].astype(jnp.int32)
            sign_x = place_ref[1, q : q + 1, :]
            hot_y = hot_ref[q]
            mixed = dot(high, hot_y) + dot(low, hot_y)
            for i in range(count):
                even = mixed[i * size_x : i * size_x + half_x]
                odd = mixed[i * size_x + half_x : (i + 1) * size_x]
                picked = jnp.where(hot_x, even + sign_x * odd, 0.0)
                value_ref[0, i, q : q + 1, :] = jnp.sum(picked, 0, keepdims=True)
        for k in range(planes):
            halves = [value_ref[0, 2 * k + i] for i in range(2)]
            halves = [jnp.concatenate([v[:, :lanes], v[:, lanes:]], 0) for v in halves]
            ride = jnp.sum(got_ref[:, k, 2 * columns :], 0, keepdims=True)
            ride = jnp.broadcast_to(ride, (lines, ride.shape[1]))
            for j in range(packs):
                spot = slice(j * columns, (j + 1) * columns)
                send_ref[pl.ds(j, lines, stride=packs), k, :] = jnp.concatenate(
                    [halves[0][:, spot], halves[1][:, spot], ride], 1
                )
        for copy in make_copies(far_ref, phase_ref, sems):
            copy.wait()


def image_kernel(
    columns,
    waves,
    small_ref,
    form_ref,
    kinetic_ref,
    strength_ref,
    phase_ref,
    table_ref,
    psi_ref,
    got_ref,
    send_ref,
):
    groups, _, rows = phase_ref.shape
    atoms = phase_ref.shape[1] // 2
    grid = table_ref.shape[1]
    owners, planes, _ = got_ref.shape
    channels = form_ref.shape[0]
    root = math.sqrt(waves)
    got = [got_ref[:, k, :] for k in range(planes)]
    ride = [g[:, 2 * columns :] for g in got]
    wide = 2 * channels
    per_row = 2 * columns // wide
    sums = jnp.concatenate(
        [r[:, wide * i : wide * (i + 1)] for r in ride[:2] for i in range(per_row)], 0
    ).T
    line = lax.broadcasted_iota(jnp.int32, (wide, channels), 0)
    spot = lax.broadcasted_iota(jnp.int32, (wide, channels), 1)
    factor = jnp.sum(
        jnp.where(lax.rem(line, channels) == spot, strength_ref[...], 0.0), 1, keepdims=True
    )
    scaled = factor * (sums / root) / root
    scaled_re = scaled[:channels].astype(bf16)
    scaled_im = scaled[channels:].astype(bf16)
    first = jnp.concatenate([scaled_re, scaled_im], 0)
    second = jnp.concatenate([scaled_im, -scaled_re], 0)
    deep = split(jnp.concatenate([g[:, : 2 * columns] for g in got], 0).T)
    by_cos = dot3(deep, (table_ref[0], table_ref[1]))
    by_sin = dot3(deep, (table_ref[2], table_ref[3]))
    out_re = by_cos[:columns] + by_sin[columns:]
    out_im = by_cos[columns:] - by_sin[:columns]
    out = jnp.concatenate(split(jnp.concatenate([out_re, out_im], 0)), 0)
    ticks = lax.broadcasted_iota(jnp.int32, (columns, rows), 0)
    depths = lax.broadcasted_iota(jnp.int32, (grid, rows), 0)
    overlap = jnp.concatenate([ride[2][:, 0:4].T, ride[2][:, 4:8].T], 1)
    for s in range(groups):
        cell = small_ref[s : s + 1, :]
        depth_hot = (depths == lax.div(cell, columns)).astype(f32).astype(bf16)
        hot = ticks == lax.rem(cell, columns)
        found = dot(out, depth_hot)
        found = found[: 2 * columns] + found[2 * columns :]
        local_re = jnp.sum(jnp.where(hot, found[:columns], 0.0), 0, keepdims=True)
        local_im = jnp.sum(jnp.where(hot, found[columns:], 0.0), 0, keepdims=True)
        form = form_ref[:, s, :]
        mixed = dot(first, phase_ref[s, 0:atoms, :]) + dot(
            second, phase_ref[s, atoms : 2 * atoms, :]
        )
        near_re = jnp.sum(form * mixed[:channels], 0, keepdims=True)
        near_im = jnp.sum(form * mixed[channels:], 0, keepdims=True)
        kinetic = kinetic_ref[s : s + 1, :]
        image_re = kinetic * two_rows(psi_ref, s, 0) + local_re + near_re
        image_im = kinetic * two_rows(psi_ref, s, 2) + local_im + near_im
        send_ref[s, 0:1, :] = image_re[:, :128]
        send_ref[s, 1:2, :] = image_re[:, 128:]
        send_ref[s, 2:3, :] = image_im[:, :128]
        send_ref[s, 3:4, :] = image_im[:, 128:]
        send_ref[s, 4:8, :] = overlap


def products_kernel(waves, basis_ref, got_ref, image_ref, send_ref):
    bands = got_ref.shape[0]
    half = basis_ref.shape[0] // 2
    owners = send_ref.shape[0]
    image_re = jnp.concatenate([got_ref[:, 0, :], got_ref[:, 1, :]], 1)
    image_im = jnp.concatenate([got_ref[:, 2, :], got_ref[:, 3, :]], 1)
    image = jnp.concatenate([image_re, image_im], 0)
    image_ref[...] = image
    mixed = dot(image, basis_ref[...], 1, 1, exact_mode) * (1.0 / waves)
    coef_re = mixed[:bands, :half] + mixed[bands:, half:]
    coef_im = mixed[bands:, :half] - mixed[:bands, half:]
    coef = jnp.concatenate([coef_re, coef_im], 1)
    own = dot(image, image, 1, 1, exact_mode) * (1.0 / waves)
    own_re = own[:bands, :bands] + own[bands:, bands:]
    own_im = own[:bands, bands:] - own[bands:, :bands]
    line = lax.broadcasted_iota(jnp.int32, (bands, bands), 0)
    spot = lax.broadcasted_iota(jnp.int32, (bands, bands), 1)
    packed = jnp.where(line <= spot, own_re, own_im)
    row = jnp.concatenate(
        [stripes(coef, bands), stripes(packed, bands), jnp.zeros((1, 128 - bands * bands), f32)], 1
    )
    send_ref[:, 0, :] = jnp.broadcast_to(row, (owners, row.shape[1]))


def overlap_kernel(waves, got_ref, over_ref):
    size = over_ref.shape[0] // 2
    packed = jnp.concatenate([got_ref[d, 4:8, :] for d in range(got_ref.shape[0])], 0)
    packed = unstripe(packed, 2) * (1.0 / waves)
    line = lax.broadcasted_iota(jnp.int32, (size, size), 0)
    spot = lax.broadcasted_iota(jnp.int32, (size, size), 1)
    turned = packed.T
    over_re = jnp.where(line <= spot, packed, turned)
    over_im = jnp.where(line < spot, -turned, jnp.where(line > spot, packed, 0.0))
    over_ref[...] = jnp.concatenate(
        [jnp.concatenate([over_re, -over_im], 1), jnp.concatenate([over_im, over_re], 1)], 0
    )


def gather_kernel(got_ref, send_ref):
    row = jnp.sum(got_ref[:, 0, :], 0, keepdims=True)
    send_ref[:, 0, :] = jnp.broadcast_to(row, (send_ref.shape[0], row.shape[1]))


def finish_kernel(
    basis_ref, image_ref, over_ref, got_ref, next_re_ref, next_im_ref, coef_re_ref, coef_im_ref, chol_re_ref, chol_im_ref
):
    bands = image_ref.shape[0] // 2
    half = basis_ref.shape[0] // 2
    row = jnp.sum(got_ref[:, 0, :], 0, keepdims=True)
    size = bands * 2 * half
    coef = unstripe(row[:, :size], bands)
    packed = unstripe(row[:, size : size + bands * bands], bands)
    coef_re = coef[:, :half]
    coef_im = coef[:, half:]
    coef_re_ref[...] = coef_re.T
    coef_im_ref[...] = coef_im.T
    line = lax.broadcasted_iota(jnp.int32, (bands, bands), 0)
    spot = lax.broadcasted_iota(jnp.int32, (bands, bands), 1)
    turned = packed.T
    own_re = jnp.where(line <= spot, packed, turned)
    own_im = jnp.where(line < spot, -turned, jnp.where(line > spot, packed, 0.0))
    left = dot(coef, over_ref[...], 1, 0, exact_mode) - 2.0 * coef
    stacked = jnp.concatenate([coef, jnp.concatenate([-coef_im, coef_re], 1)], 0)
    mixed = dot(stacked, left, 1, 1, exact_mode)
    gram_re = own_re + mixed[:bands]
    gram_im = own_im + mixed[bands:]
    eye = jnp.where(line == spot, 1.0, 0.0)
    work_re = jnp.concatenate([gram_re, eye], 1)
    work_im = jnp.concatenate([gram_im, jnp.zeros_like(eye)], 1)
    rows_re, rows_im = [], []
    for k in range(bands):
        pivot = lax.rsqrt(work_re[k : k + 1, k : k + 1])
        lead_re = work_re[k : k + 1, :] * pivot
        lead_im = work_im[k : k + 1, :] * pivot
        rows_re.append(lead_re)
        rows_im.append(lead_im)
        if k + 1 < bands:
            column_re = work_re[:, k : k + 1] * pivot
            column_im = work_im[:, k : k + 1] * pivot
            work_re, work_im = (
                work_re - (column_re * lead_re - column_im * lead_im),
                work_im - (column_re * lead_im + column_im * lead_re),
            )
    all_re = jnp.concatenate(rows_re, 0)
    all_im = jnp.concatenate(rows_im, 0)
    chol_re_ref[...] = jnp.where(line <= spot, all_re[:, :bands], 0.0)
    chol_im_ref[...] = jnp.where(line < spot, all_im[:, :bands], 0.0)
    inv_re = all_re[:, bands:]
    inv_im = all_im[:, bands:]
    basis_re = basis_ref[0:half, :]
    basis_im = basis_ref[half : 2 * half, :]
    span_re = dot(coef, jnp.concatenate([basis_re, -basis_im], 0), 1, 0, exact_mode)
    span_im = dot(coef, jnp.concatenate([basis_im, basis_re], 0), 1, 0, exact_mode)
    rest_re = image_ref[0:bands, :] - span_re
    rest_im = image_ref[bands : 2 * bands, :] - span_im
    next_re = dot(inv_re, rest_re, 1, 0, exact_mode) + dot(inv_im, rest_im, 1, 0, exact_mode)
    next_im = dot(inv_re, rest_im, 1, 0, exact_mode) - dot(inv_im, rest_re, 1, 0, exact_mode)
    for ref, value in ((next_re_ref, next_re), (next_im_ref, next_im)):
        ref[pl.ds(0, bands, stride=2), :] = value[:, :128]
        ref[pl.ds(1, bands, stride=2), :] = value[:, 128:]


def body(
    basis_re,
    basis_im,
    potential,
    kinetic,
    form_factors,
    channel_strength,
    sphere_map,
    column_map,
    atom_sites,
):
    blocks, slab, _, row_count = basis_re.shape
    band_count = lax.axis_size("band")
    owners = lax.axis_size("pw")
    planes, grid, _ = potential.shape
    columns = column_map.shape[0] // owners
    waves = band_count * owners * row_count
    atoms = atom_sites.shape[1]
    rows = blocks * slab
    half_x, half_y = grid // 2 + 8, 128
    tables = transform_tables(grid, planes, half_x, half_y)
    owner_table, table_x, table_y = [jnp.asarray(table) for table in tables]

    def exchange(part, axis, groups=None):
        return lax.all_to_all(
            part, axis, split_axis=0, concat_axis=0, axis_index_groups=groups, tiled=True
        )

    near, far = {}, {}
    for z in range(band_count):
        for p in range(owners):
            y, rest = divmod(p, 8)
            near.setdefault((z // 2, y // 2), []).append(z * owners + p)
            far.setdefault((z % 2, y % 2, rest), []).append(z * owners + p)
    near, far = list(near.values()), list(far.values())

    places = column_map.reshape(-1, 128)
    basis, send, small = kernel_call(
        pack_kernel,
        (
            shape(2 * rows, row_count),
            shape(slab, 8, 128),
            shape(3 * 8, row_count, dtype=jnp.int32),
        ),
        basis_re.reshape(-1, 128),
        basis_im.reshape(-1, 128),
        sphere_map,
        places,
        atom_sites,
        scratch=(
            pltpu.VMEM((2 * rows, 128), f32),
            pltpu.VMEM((2 * rows, 128), f32),
            pltpu.VMEM(sphere_map.shape, jnp.int32),
            pltpu.VMEM(places.shape, jnp.int32),
            pltpu.VMEM(atom_sites.shape, jnp.int32),
            pltpu.SemaphoreType.DMA((2, 4)),
            pltpu.SemaphoreType.DMA((3,)),
        ),
        far=(0, 1, 2, 3, 4),
        vmem=63,
    )
    psi = exchange(send, "band")

    phase_dims = (band_count, 2 * atoms, row_count)
    phase_sems = (pltpu.SemaphoreType.DMA((band_count,)),)
    phase_scratch = (pltpu.VMEM(phase_dims, bf16),) + phase_sems
    far_phase = kernel_call(
        lambda *refs: phase_kernel(grid, columns, *refs),
        shape(16 * band_count, *phase_dims[1:], dtype=bf16),
        small,
        scratch=phase_scratch,
        far_out=(0,),
        vmem=8,
        flops=10**7,
    )
    send = kernel_call(
        lambda *refs: columns_kernel(columns, *refs),
        shape(owners, planes, 128),
        small,
        form_factors,
        far_phase,
        owner_table,
        psi,
        scratch=phase_scratch,
        far=(2,),
    )
    got = exchange(send, "pw")
    folded = kernel_call(fold_kernel, shape(planes, 2 * half_x, 2 * half_y), potential)
    send, phase = kernel_call(
        lambda *refs: planes_kernel(columns, grid, *refs),
        (shape(owners, planes, 128), shape(*phase_dims, dtype=bf16)),
        small,
        folded,
        table_x,
        table_y,
        far_phase,
        got,
        scratch=phase_sems
        + (
            pltpu.VMEM((2, 4 * planes, 8, row_count), f32),
            pltpu.VMEM((4, 8, row_count), f32),
            pltpu.VMEM((8, 2 * half_y, row_count), bf16),
            pltpu.VMEM((4 * planes * half_x, 2 * half_y), f32),
        ),
        grid=(3,),
        far=(4,),
        vmem=16,
    )
    got = exchange(send, "pw")
    send = kernel_call(
        lambda *refs: image_kernel(columns, waves, *refs),
        shape(band_count, 8, 128),
        small,
        form_factors,
        kinetic,
        channel_strength[None, :],
        phase,
        owner_table,
        psi,
        got,
    )
    got = exchange(send, "band")
    image, send = kernel_call(
        lambda *refs: products_kernel(waves, *refs),
        (shape(2 * slab, row_count), shape(len(near[0]), 1, 9 * 128)),
        basis,
        got,
    )
    over = kernel_call(
        lambda *refs: overlap_kernel(waves, *refs), shape(2 * rows, 2 * rows), got
    )
    got = exchange(send, ("band", "pw"), near)
    send = kernel_call(gather_kernel, shape(len(far[0]), 1, 9 * 128), got)
    got = exchange(send, ("band", "pw"), far)
    next_re, next_im, coef_re, coef_im, chol_re, chol_im = kernel_call(
        finish_kernel,
        (
            shape(2 * slab, 128),
            shape(2 * slab, 128),
            shape(rows, slab),
            shape(rows, slab),
            shape(slab, slab),
            shape(slab, slab),
        ),
        basis,
        image,
        over,
        got,
    )
    return (
        next_re.reshape(slab, 1, row_count),
        next_im.reshape(slab, 1, row_count),
        coef_re.reshape(blocks, slab, slab),
        coef_im.reshape(blocks, slab, slab),
        chol_re,
        chol_im,
    )


def solution(mesh):
    return jax.shard_map(
        body,
        mesh=mesh,
        in_specs=(
            P(None, None, "band", "pw"),
            P(None, None, "band", "pw"),
            P("pw", None, None),
            P(None, "pw"),
            P(None, None, "pw"),
            P(),
            P(None, "pw"),
            P(),
            P(),
        ),
        out_specs=(P(None, "band", "pw"), P(None, "band", "pw"), P(), P(), P(), P()),
        check_vma=False,
    )
```

```python
import math

import jax
import jax.numpy as jnp
import numpy as np
from jax import lax
from jax.experimental import pallas as pl
from jax.experimental.pallas import tpu as pltpu
from jax.sharding import PartitionSpec as P

f32 = jnp.float32
bf16 = jnp.bfloat16
exact_mode = lax.Precision.HIGHEST

COS_POLY = (0.9999999403953552, -4.934792995452881, 4.058411121368408, -1.331876516342163, 0.21968960762023926)
SIN_POLY = (3.1415903568267822, -5.1674065589904785, 2.5440104007720947, -0.5594624280929565)
WHOLE = 1.5 * 2.0**23


def dot(left, right, left_dim=1, right_dim=0, precision=None):
    return lax.dot_general(
        left,
        right,
        (((left_dim,), (right_dim,)), ((), ())),
        precision=precision,
        preferred_element_type=f32,
    )


def split(part):
    high = part.astype(bf16)
    return high, (part - high.astype(f32)).astype(bf16)


def split3(part):
    high = part.astype(bf16)
    rest = part - high.astype(f32)
    middle = rest.astype(bf16)
    return [high, middle, (rest - middle.astype(f32)).astype(bf16)]


def dot3(left, right, left_dim=1, right_dim=0):
    lh, ll = left
    rh, rl = right
    return (
        dot(lh, rh, left_dim, right_dim)
        + dot(ll, rh, left_dim, right_dim)
        + dot(lh, rl, left_dim, right_dim)
    )


def pieces(table):
    table = table.astype(np.float32)
    high = table.astype(jnp.bfloat16)
    return [high, (table - high.astype(np.float32)).astype(jnp.bfloat16)]


def transform_tables(grid, planes, half_x, half_y):
    cos = np.array([math.cos(2.0 * math.pi * t / grid) for t in range(grid)])
    sin = np.array([math.sin(2.0 * math.pi * t / grid) for t in range(grid)])
    ticks = np.arange(grid)
    turns = ticks[:, None] * ticks[None, :] % grid
    order = ticks.reshape(grid // planes, planes).T.reshape(-1)
    by_owner = np.stack(pieces(cos[turns[order]]) + pieces(sin[turns[order]]))
    top = grid // 2 + 1

    def folded(half):
        table = np.zeros((2 * half, 2 * half))
        table[:top, :top] = cos[turns[:top, :top]]
        table[half + 1 : half + top - 1, half + 1 : half + top - 1] = sin[
            turns[1 : top - 1, 1 : top - 1]
        ]
        return pieces(table)

    high, low = folded(half_x)
    table_x = np.concatenate([high, low, high], 1)
    high, low = folded(half_y)
    table_y = np.concatenate([high, high, low], 0)
    return by_owner, table_x, table_y


def stripes(part, count):
    rows = part.shape[0] // count
    return jnp.concatenate([part[i * rows : (i + 1) * rows] for i in range(count)], 1)


def unstripe(part, count):
    width = part.shape[1] // count
    return jnp.concatenate([part[:, i * width : (i + 1) * width] for i in range(count)], 0)


def kernel_call(kernel, outs, *args, flops=10**6, vmem=8, scratch=(), far=(), far_out=(), grid=()):
    single = not isinstance(outs, tuple)
    outs = (outs,) if single else outs
    place = (pl.BlockSpec(memory_space=pltpu.VMEM), pl.BlockSpec(memory_space=pltpu.HBM))
    out = pl.pallas_call(
        kernel,
        out_shape=outs,
        in_specs=[place[i in far] for i in range(len(args))],
        scratch_shapes=scratch,
        grid=grid,
        out_specs=tuple(place[i in far_out] for i in range(len(outs))),
        compiler_params=pltpu.CompilerParams(vmem_limit_bytes=vmem * 2**20),
        cost_estimate=pl.CostEstimate(flops=flops, bytes_accessed=4 * 10**6, transcendentals=0),
    )(*args)
    return out[0] if single else out


def shape(*dims, dtype=f32):
    return jax.ShapeDtypeStruct(dims, dtype)


def pack_kernel(
    far_re_ref,
    far_im_ref,
    far_map_ref,
    far_place_ref,
    far_sites_ref,
    basis_ref,
    send_ref,
    small_ref,
    re_ref,
    im_ref,
    map_ref,
    place_ref,
    sites_ref,
    sems,
    small_sems,
):
    count = sems.shape[1]
    small = [
        pltpu.make_async_copy(far, near, small_sems.at[i])
        for i, (far, near) in enumerate(
            ((far_map_ref, map_ref), (far_place_ref, place_ref), (far_sites_ref, sites_ref))
        )
    ]
    size = re_ref.shape[0] // count
    copies = [
        pltpu.make_async_copy(
            far.at[pl.ds(i * size, size)], near.at[pl.ds(i * size, size)], sems.at[part, i]
        )
        for part, (far, near) in enumerate(((far_re_ref, re_ref), (far_im_ref, im_ref)))
        for i in range(count)
    ]
    for copy in copies + small:
        copy.start()
    for copy in copies + small:
        copy.wait()
    count = map_ref.shape[0]
    lines = place_ref.shape[0] // 2
    small_ref[0:count, :] = map_ref[...]
    small_ref[count : count + lines, :] = jnp.concatenate(
        [place_ref[0:lines, :], place_ref[lines:, :]], 1
    )
    small_ref[count + lines :, :] = jnp.concatenate(
        [
            sites_ref[:, 0 : small_ref.shape[1]],
            sites_ref[:, small_ref.shape[1] :],
            jnp.zeros((2, small_ref.shape[1]), jnp.int32),
        ],
        0,
    )
    rows = re_ref.shape[0] // 2
    bands = send_ref.shape[0]

    def whole(ref):
        return jnp.concatenate(
            [ref[pl.ds(0, rows, stride=2), :], ref[pl.ds(1, rows, stride=2), :]], 1
        )

    basis = jnp.concatenate([whole(re_ref), whole(im_ref)], 0)
    basis_ref[...] = basis
    mixed = dot(basis, basis, 1, 1, exact_mode)
    over_re = mixed[:rows, :rows] + mixed[rows:, rows:]
    over_im = mixed[:rows, rows:] - mixed[rows:, :rows]
    line = lax.broadcasted_iota(jnp.int32, (rows, rows), 0)
    spot = lax.broadcasted_iota(jnp.int32, (rows, rows), 1)
    packed = stripes(jnp.where(line <= spot, over_re, over_im), 2)
    first = 2 * (rows - bands)
    for band in range(bands):
        send_ref[band, 0:2, :] = re_ref[first + 2 * band : first + 2 * band + 2, :]
        send_ref[band, 2:4, :] = im_ref[first + 2 * band : first + 2 * band + 2, :]
        send_ref[band, 4:8, :] = packed[4 * band : 4 * band + 4, :]


def phase_kernel(grid, columns, small_ref, far_ref, phase_ref, sems):
    groups, _, rows = phase_ref.shape
    atoms = phase_ref.shape[1] // 2
    copies = [
        pltpu.make_async_copy(phase_ref.at[s], far_ref.at[s], sems.at[s]) for s in range(groups)
    ]
    root = math.sqrt(2.0)
    cos_poly = [root * c / grid ** (2 * k) for k, c in enumerate(COS_POLY)]
    sin_poly = [root * c / grid ** (2 * k + 1) for k, c in enumerate(SIN_POLY)]
    sites = jnp.concatenate([small_ref[16:19, :], small_ref[19:22, :]], 1).astype(f32)
    sites = jnp.concatenate([sites, jnp.zeros((5, atoms), f32)], 0).astype(bf16)
    owner = lax.axis_index("pw")
    packs = rows // columns
    row = lax.div(owner, packs // 2)
    line = small_ref[pl.ds(groups + lax.rem(row, groups), 1), :]
    block = lax.div(row, groups) * (packs // 2) + lax.rem(owner, packs // 2)
    mine = jnp.zeros((1, columns), jnp.int32)
    for j in range(packs):
        chosen = (block == j).astype(jnp.int32)
        mine = mine + chosen * line[:, j * columns : (j + 1) * columns]
    mine = jnp.concatenate([mine, jnp.zeros((7, columns), jnp.int32)], 0).T[:, 0:1]
    column_x = lax.div(mine, grid).astype(f32)
    column_y = lax.rem(mine, grid).astype(f32)
    ticks = lax.broadcasted_iota(jnp.int32, (columns, rows), 0)
    for s in range(groups):
        cell = small_ref[s : s + 1, :]
        depth = lax.div(cell, columns).astype(f32)
        hot = ticks == lax.rem(cell, columns)
        x = jnp.sum(jnp.where(hot, column_x, 0.0), 0, keepdims=True)
        y = jnp.sum(jnp.where(hot, column_y, 0.0), 0, keepdims=True)
        place = jnp.concatenate([depth, x, y, jnp.zeros((5, rows), f32)], 0).astype(bf16)
        turns = dot(sites, place, 0, 0)
        turns = turns - grid * ((turns * (1.0 / grid) + WHOLE) - WHOLE)
        w = turns * turns
        c = cos_poly[-1]
        for value in cos_poly[-2::-1]:
            c = c * w + value
        h = sin_poly[-1]
        for value in sin_poly[-2::-1]:
            h = h * w + value
        h = h * turns
        phase_ref[s, 0:atoms, :] = (1.0 - h * h).astype(bf16)
        phase_ref[s, atoms : 2 * atoms, :] = (h * c).astype(bf16)
        copies[s].start()
    for copy in copies:
        copy.wait()


def two_rows(ref, s, line):
    return jnp.concatenate([ref[s, line : line + 1, :], ref[s, line + 1 : line + 2, :]], 1)


def make_copies(far_ref, near_ref, sems, first=0):
    return [
        pltpu.make_async_copy(far_ref.at[first + i], near_ref.at[i], sems.at[i])
        for i in range(near_ref.shape[0])
    ]


def fetch(far_ref, near_ref, sems, first=0):
    copies = make_copies(far_ref, near_ref, sems, first)
    for copy in copies:
        copy.start()
    return copies


def fold(pot_ref, out_ref):
    planes, grid, _ = pot_ref.shape

    def chooser(size):
        half = size // 2
        line = lax.broadcasted_iota(jnp.int32, (size, grid), 0)
        spot = lax.broadcasted_iota(jnp.int32, (size, grid), 1)
        t = jnp.where(line < half, line, line - half)
        plus = (line < half) & (t <= grid // 2) & (spot == t)
        minus = (line >= half) & (t > 0) & (t < grid // 2) & (spot == grid - t)
        return jnp.where(plus | minus, 1.0, 0.0).astype(bf16)

    lines = chooser(out_ref.shape[1])
    spots = chooser(out_ref.shape[2])
    for k in range(planes):
        part = sum(dot(lines, piece) for piece in split(pot_ref[k]))
        part = sum(dot(piece, spots, 1, 1) for piece in split(part))
        out_ref[k] = part * (1.0 / grid**3)


def columns_kernel(
    columns,
    small_ref,
    form_ref,
    far_ref,
    table_ref,
    pot_ref,
    got_ref,
    send_ref,
    fold_ref,
    phase_ref,
    sems,
    first_ref,
    second_ref,
):
    groups, _, rows = phase_ref.shape
    atoms = phase_ref.shape[1] // 2
    grid = table_ref.shape[1]
    owners, planes, _ = send_ref.shape
    channels = form_ref.shape[0]
    step = pl.program_id(0)

    @pl.when(step == 0)
    def to_depth():
        fetch(far_ref, phase_ref, sems)
        ticks = lax.broadcasted_iota(jnp.int32, (columns, rows), 0)
        deep = lax.broadcasted_iota(jnp.int32, (grid, rows), 0)
        total = jnp.zeros((4 * columns, grid), f32)
        for s in range(groups):
            psi_re = two_rows(got_ref, s, 0)
            psi_im = two_rows(got_ref, s, 2)
            cell = small_ref[s : s + 1, :]
            depth_hot = (deep == lax.div(cell, columns)).astype(f32).astype(bf16)
            hot = ticks == lax.rem(cell, columns)
            spread = jnp.concatenate(
                [jnp.where(hot, psi_re, 0.0), jnp.where(hot, psi_im, 0.0)], 0
            )
            total = total + dot(jnp.concatenate(split(spread), 0), depth_hot, 1, 1)
            form = form_ref[:, s, :]
            weighted_re = (form * psi_re).astype(bf16)
            weighted_im = (form * psi_im).astype(bf16)
            first_ref[s] = jnp.concatenate([weighted_re, weighted_im], 0)
            second_ref[s] = jnp.concatenate([-weighted_im, weighted_re], 0)
        column = split(total[: 2 * columns] + total[2 * columns :])
        by_cos = dot3((table_ref[0], table_ref[1]), column, 1, 1)
        by_sin = dot3((table_ref[2], table_ref[3]), column, 1, 1)
        deep_re = by_cos[:, :columns] - by_sin[:, columns:]
        deep_im = by_sin[:, :columns] + by_cos[:, columns:]
        for k in range(planes):
            lines = slice(owners * k, owners * (k + 1))
            send_ref[:, k, 0 : 2 * columns] = jnp.concatenate([deep_re[lines], deep_im[lines]], 1)
        fold(pot_ref, fold_ref)

    @pl.when(step == 1)
    def to_products():
        products = jnp.zeros((atoms, 2 * channels), f32)
        copies = make_copies(far_ref, phase_ref, sems)
        for s in range(groups):
            copies[s].wait()
            products = products + (
                dot(phase_ref[s, 0:atoms, :], first_ref[s], 1, 1)
                + dot(phase_ref[s, atoms : 2 * atoms, :], second_ref[s], 1, 1)
            )
        parts = [products[owners * k : owners * (k + 1)] for k in range(atoms // owners)]
        half = len(parts) // 2
        overlap = jnp.sum(got_ref[:, 4:8, :], 0).T
        own = jnp.concatenate(
            [overlap[:owners], overlap[owners:], jnp.zeros((owners, 2 * columns - 8), f32)], 1
        )
        extra = [jnp.concatenate(parts[:half], 1), jnp.concatenate(parts[half:], 1), own]
        for k in range(planes):
            send_ref[:, k, 2 * columns :] = extra[k]


def planes_kernel(
    columns,
    grid,
    small_ref,
    fold_ref,
    table_x_ref,
    table_y_ref,
    far_ref,
    got_ref,
    send_ref,
    phase_ref,
    sems,
    value_ref,
    place_ref,
    hot_ref,
    field_ref,
):
    planes, size_x, size_y = fold_ref.shape
    half_x, half_y = size_x // 2, size_y // 2
    owners = got_ref.shape[0]
    steps, _, wide = phase_ref.shape
    lines, lanes = 2 * steps, wide // 2
    packs = lanes // columns
    ticks_x = lax.broadcasted_iota(jnp.int32, (half_x, wide), 0)
    ticks_y = lax.broadcasted_iota(jnp.int32, (half_y, wide), 0)
    count = 2 * planes

    def folded(at):
        t = jnp.minimum(at, grid - at)
        sign = jnp.where(at == t, 1.0, -1.0)
        return t.astype(f32), jnp.where((t == 0) | (2 * t == grid), 0.0, sign)

    def along_y(part):
        high, low = split(part)
        return dot(jnp.concatenate([high, low, high], 1), table_y_ref[...])

    def along_x(part):
        high, low = split(part)
        return dot(table_x_ref[...], jnp.concatenate([high, high, low], 0))

    def quarters(part):
        return (
            part[:half_x, :half_y],
            part[:half_x, half_y:],
            part[half_x:, :half_y],
            part[half_x:, half_y:],
        )

    def join(ee, eo, oe, oo):
        return jnp.concatenate(
            [jnp.concatenate([ee, eo], 1), jnp.concatenate([oe, oo], 1)], 0
        )

    step = pl.program_id(0)

    @pl.when(step == 0)
    def to_planes():
        fetch(far_ref, phase_ref, sems)
        place = small_ref[steps : 2 * steps, :]
        for i, at in enumerate((lax.div(place, grid), lax.rem(place, grid))):
            place_ref[2 * i], place_ref[2 * i + 1] = folded(at)
        for k in range(planes):
            loaded = [got_ref[pl.ds(j, lines, stride=packs), k, :] for j in range(packs)]
            for part in range(2):
                spot = slice(part * columns, (part + 1) * columns)
                value = jnp.concatenate([v[:, spot] for v in loaded], 1)
                value = jnp.concatenate([value[:steps], value[steps:]], 1)
                for piece, half in enumerate(split(value)):
                    half = half.astype(f32)
                    value_ref[piece, 2 * (2 * k + part)] = half
                    value_ref[piece, 2 * (2 * k + part) + 1] = half * place_ref[1]
        field = jnp.zeros((count * size_x, size_y), f32)
        for q in range(steps):
            hot_x = ticks_x == place_ref[0, q : q + 1, :].astype(jnp.int32)
            hot_y = ticks_y == place_ref[2, q : q + 1, :].astype(jnp.int32)
            hot_y = jnp.concatenate(
                [jnp.where(hot_y, 1.0, 0.0), jnp.where(hot_y, place_ref[3, q : q + 1, :], 0.0)], 0
            ).astype(bf16)
            hot_ref[q] = hot_y
            for piece in range(2):
                spread = [
                    jnp.where(hot_x, value_ref[piece, i, q : q + 1, :], 0.0) for i in range(2 * count)
                ]
                field = field + dot(jnp.concatenate(spread, 0).astype(bf16), hot_y, 1, 1)
        field_ref[...] = field

    @pl.when(step == 1)
    def transforms():
        field = along_y(field_ref[...])
        back = []
        for k in range(planes):
            re, im = [
                quarters(along_x(field[(2 * k + i) * size_x : (2 * k + i + 1) * size_x]))
                for i in range(2)
            ]
            values_v = quarters(fold_ref[k])
            real_sum, real_gap = re[0] - re[3], re[0] + re[3]
            imag_sum, imag_gap = im[0] - im[3], im[0] + im[3]
            cross_re, cross_re_gap = re[1] + re[2], re[1] - re[2]
            cross_im, cross_im_gap = im[1] + im[2], im[1] - im[2]
            pp_re, mm_re = real_sum - cross_im, real_sum + cross_im
            pp_im, mm_im = imag_sum + cross_re, imag_sum - cross_re
            pm_re, mp_re = real_gap + cross_im_gap, real_gap - cross_im_gap
            pm_im, mp_im = imag_gap - cross_re_gap, imag_gap + cross_re_gap
            parts = []
            for pp, pm, mp, mm in (
                (pp_re, pm_re, mp_re, mm_re),
                (pp_im, pm_im, mp_im, mm_im),
            ):
                pp, pm, mp, mm = [a * b for a, b in zip((pp, pm, mp, mm), values_v)]
                plus_s, plus_g = pp + pm, pp - pm
                minus_s, minus_g = mp + mm, mp - mm
                parts.append((plus_s + minus_s, plus_g + minus_g, plus_s - minus_s, plus_g - minus_g))
            re, im = parts
            back.append(along_x(join(re[0], im[1], im[2], -re[3])))
            back.append(along_x(join(im[0], -re[1], -re[2], -im[3])))
        field_ref[...] = along_y(jnp.concatenate(back, 0))

    @pl.when(step == 2)
    def to_columns():
        high, low = split(field_ref[...])
        for q in range(steps):
            hot_x = ticks_x == place_ref[0, q : q + 1, :].astype(jnp.int32)
            sign_x = place_ref[1, q : q + 1, :]
            hot_y = hot_ref[q]
            mixed = dot(high, hot_y) + dot(low, hot_y)
            for i in range(count):
                even = mixed[i * size_x : i * size_x + half_x]
                odd = mixed[i * size_x + half_x : (i + 1) * size_x]
                picked = jnp.where(hot_x, even + sign_x * odd, 0.0)
                value_ref[0, i, q : q + 1, :] = jnp.sum(picked, 0, keepdims=True)
        for k in range(planes):
            halves = [value_ref[0, 2 * k + i] for i in range(2)]
            halves = [jnp.concatenate([v[:, :lanes], v[:, lanes:]], 0) for v in halves]
            ride = jnp.sum(got_ref[:, k, 2 * columns :], 0, keepdims=True)
            ride = jnp.broadcast_to(ride, (lines, ride.shape[1]))
            for j in range(packs):
                spot = slice(j * columns, (j + 1) * columns)
                send_ref[pl.ds(j, lines, stride=packs), k, :] = jnp.concatenate(
                    [halves[0][:, spot], halves[1][:, spot], ride], 1
                )
        for copy in make_copies(far_ref, phase_ref, sems):
            copy.wait()


def image_kernel(
    columns,
    waves,
    small_ref,
    form_ref,
    kinetic_ref,
    strength_ref,
    phase_ref,
    table_ref,
    psi_ref,
    got_ref,
    send_ref,
):
    groups, _, rows = phase_ref.shape
    atoms = phase_ref.shape[1] // 2
    grid = table_ref.shape[1]
    owners, planes, _ = got_ref.shape
    channels = form_ref.shape[0]
    root = math.sqrt(waves)
    got = [got_ref[:, k, :] for k in range(planes)]
    ride = [g[:, 2 * columns :] for g in got]
    wide = 2 * channels
    per_row = 2 * columns // wide
    sums = jnp.concatenate(
        [r[:, wide * i : wide * (i + 1)] for r in ride[:2] for i in range(per_row)], 0
    ).T
    line = lax.broadcasted_iota(jnp.int32, (wide, channels), 0)
    spot = lax.broadcasted_iota(jnp.int32, (wide, channels), 1)
    factor = jnp.sum(
        jnp.where(lax.rem(line, channels) == spot, strength_ref[...], 0.0), 1, keepdims=True
    )
    scaled = factor * (sums / root) / root
    scaled_re = scaled[:channels].astype(bf16)
    scaled_im = scaled[channels:].astype(bf16)
    first = jnp.concatenate([scaled_re, scaled_im], 0)
    second = jnp.concatenate([scaled_im, -scaled_re], 0)
    deep = split(jnp.concatenate([g[:, : 2 * columns] for g in got], 0).T)
    by_cos = dot3(deep, (table_ref[0], table_ref[1]))
    by_sin = dot3(deep, (table_ref[2], table_ref[3]))
    out_re = by_cos[:columns] + by_sin[columns:]
    out_im = by_cos[columns:] - by_sin[:columns]
    out = jnp.concatenate(split(jnp.concatenate([out_re, out_im], 0)), 0)
    ticks = lax.broadcasted_iota(jnp.int32, (columns, rows), 0)
    depths = lax.broadcasted_iota(jnp.int32, (grid, rows), 0)
    overlap = jnp.concatenate([ride[2][:, 0:4].T, ride[2][:, 4:8].T], 1)
    for s in range(groups):
        cell = small_ref[s : s + 1, :]
        depth_hot = (depths == lax.div(cell, columns)).astype(f32).astype(bf16)
        hot = ticks == lax.rem(cell, columns)
        found = dot(out, depth_hot)
        found = found[: 2 * columns] + found[2 * columns :]
        local_re = jnp.sum(jnp.where(hot, found[:columns], 0.0), 0, keepdims=True)
        local_im = jnp.sum(jnp.where(hot, found[columns:], 0.0), 0, keepdims=True)
        form = form_ref[:, s, :]
        mixed = dot(first, phase_ref[s, 0:atoms, :]) + dot(
            second, phase_ref[s, atoms : 2 * atoms, :]
        )
        near_re = jnp.sum(form * mixed[:channels], 0, keepdims=True)
        near_im = jnp.sum(form * mixed[channels:], 0, keepdims=True)
        kinetic = kinetic_ref[s : s + 1, :]
        image_re = kinetic * two_rows(psi_ref, s, 0) + local_re + near_re
        image_im = kinetic * two_rows(psi_ref, s, 2) + local_im + near_im
        send_ref[s, 0:1, :] = image_re[:, :128]
        send_ref[s, 1:2, :] = image_re[:, 128:]
        send_ref[s, 2:3, :] = image_im[:, :128]
        send_ref[s, 3:4, :] = image_im[:, 128:]
        send_ref[s, 4:8, :] = overlap


def overlap(waves, got_ref, over_ref):
    size = over_ref.shape[0] // 2
    packed = jnp.concatenate([got_ref[d, 4:8, :] for d in range(got_ref.shape[0])], 0)
    packed = unstripe(packed, 2) * (1.0 / waves)
    line = lax.broadcasted_iota(jnp.int32, (size, size), 0)
    spot = lax.broadcasted_iota(jnp.int32, (size, size), 1)
    turned = packed.T
    over_re = jnp.where(line <= spot, packed, turned)
    over_im = jnp.where(line < spot, -turned, jnp.where(line > spot, packed, 0.0))
    over_ref[...] = jnp.concatenate(
        [jnp.concatenate([over_re, -over_im], 1), jnp.concatenate([over_im, over_re], 1)], 0
    )


def products_kernel(waves, basis_ref, got_ref, image_ref, over_ref, send_ref):
    overlap(waves, got_ref, over_ref)
    bands = got_ref.shape[0]
    half = basis_ref.shape[0] // 2
    owners = send_ref.shape[0]
    image_re = jnp.concatenate([got_ref[:, 0, :], got_ref[:, 1, :]], 1)
    image_im = jnp.concatenate([got_ref[:, 2, :], got_ref[:, 3, :]], 1)
    image = jnp.concatenate([image_re, image_im], 0)
    image_ref[...] = image
    mixed = dot(image, basis_ref[...], 1, 1, exact_mode) * (1.0 / waves)
    coef_re = mixed[:bands, :half] + mixed[bands:, half:]
    coef_im = mixed[bands:, :half] - mixed[:bands, half:]
    coef = jnp.concatenate([coef_re, coef_im], 1)
    own = dot(image, image, 1, 1, exact_mode) * (1.0 / waves)
    own_re = own[:bands, :bands] + own[bands:, bands:]
    own_im = own[:bands, bands:] - own[bands:, :bands]
    line = lax.broadcasted_iota(jnp.int32, (bands, bands), 0)
    spot = lax.broadcasted_iota(jnp.int32, (bands, bands), 1)
    packed = jnp.where(line <= spot, own_re, own_im)
    row = jnp.concatenate(
        [stripes(coef, bands), stripes(packed, bands), jnp.zeros((1, 128 - bands * bands), f32)], 1
    )
    send_ref[:, 0, :] = jnp.broadcast_to(row, (owners, row.shape[1]))


def gather_kernel(got_ref, send_ref):
    row = jnp.sum(got_ref[:, 0, :], 0, keepdims=True)
    send_ref[:, 0, :] = jnp.broadcast_to(row, (send_ref.shape[0], row.shape[1]))


def finish_kernel(
    basis_ref, image_ref, over_ref, got_ref, next_re_ref, next_im_ref, coef_re_ref, coef_im_ref, chol_re_ref, chol_im_ref
):
    bands = image_ref.shape[0] // 2
    half = basis_ref.shape[0] // 2
    row = jnp.sum(got_ref[:, 0, :], 0, keepdims=True)
    size = bands * 2 * half
    coef = unstripe(row[:, :size], bands)
    packed = unstripe(row[:, size : size + bands * bands], bands)
    coef_re = coef[:, :half]
    coef_im = coef[:, half:]
    coef_re_ref[...] = coef_re.T
    coef_im_ref[...] = coef_im.T
    line = lax.broadcasted_iota(jnp.int32, (bands, bands), 0)
    spot = lax.broadcasted_iota(jnp.int32, (bands, bands), 1)
    turned = packed.T
    own_re = jnp.where(line <= spot, packed, turned)
    own_im = jnp.where(line < spot, -turned, jnp.where(line > spot, packed, 0.0))
    left = dot(coef, over_ref[...], 1, 0, exact_mode) - 2.0 * coef
    stacked = jnp.concatenate([coef, jnp.concatenate([-coef_im, coef_re], 1)], 0)
    mixed = dot(stacked, left, 1, 1, exact_mode)
    gram_re = own_re + mixed[:bands]
    gram_im = own_im + mixed[bands:]
    eye = jnp.where(line == spot, 1.0, 0.0)
    work_re = jnp.concatenate([gram_re, eye], 1)
    work_im = jnp.concatenate([gram_im, jnp.zeros_like(eye)], 1)
    rows_re, rows_im = [], []
    for k in range(bands):
        pivot = lax.rsqrt(work_re[k : k + 1, k : k + 1])
        lead_re = work_re[k : k + 1, :] * pivot
        lead_im = work_im[k : k + 1, :] * pivot
        rows_re.append(lead_re)
        rows_im.append(lead_im)
        if k + 1 < bands:
            column_re = work_re[:, k : k + 1] * pivot
            column_im = work_im[:, k : k + 1] * pivot
            work_re, work_im = (
                work_re - (column_re * lead_re - column_im * lead_im),
                work_im - (column_re * lead_im + column_im * lead_re),
            )
    all_re = jnp.concatenate(rows_re, 0)
    all_im = jnp.concatenate(rows_im, 0)
    chol_re_ref[...] = jnp.where(line <= spot, all_re[:, :bands], 0.0)
    chol_im_ref[...] = jnp.where(line < spot, all_im[:, :bands], 0.0)
    inv_re = all_re[:, bands:]
    inv_im = all_im[:, bands:]
    basis_re = basis_ref[0:half, :]
    basis_im = basis_ref[half : 2 * half, :]
    span_re = dot(coef, jnp.concatenate([basis_re, -basis_im], 0), 1, 0, exact_mode)
    span_im = dot(coef, jnp.concatenate([basis_im, basis_re], 0), 1, 0, exact_mode)
    rest_re = image_ref[0:bands, :] - span_re
    rest_im = image_ref[bands : 2 * bands, :] - span_im
    next_re = dot(inv_re, rest_re, 1, 0, exact_mode) + dot(inv_im, rest_im, 1, 0, exact_mode)
    next_im = dot(inv_re, rest_im, 1, 0, exact_mode) - dot(inv_im, rest_re, 1, 0, exact_mode)
    for ref, value in ((next_re_ref, next_re), (next_im_ref, next_im)):
        ref[pl.ds(0, bands, stride=2), :] = value[:, :128]
        ref[pl.ds(1, bands, stride=2), :] = value[:, 128:]


def body(
    basis_re,
    basis_im,
    potential,
    kinetic,
    form_factors,
    channel_strength,
    sphere_map,
    column_map,
    atom_sites,
):
    blocks, slab, _, row_count = basis_re.shape
    band_count = lax.axis_size("band")
    owners = lax.axis_size("pw")
    planes, grid, _ = potential.shape
    columns = column_map.shape[0] // owners
    waves = band_count * owners * row_count
    atoms = atom_sites.shape[1]
    rows = blocks * slab
    half_x, half_y = grid // 2 + 8, 128
    tables = transform_tables(grid, planes, half_x, half_y)
    owner_table, table_x, table_y = [jnp.asarray(table) for table in tables]

    def exchange(part, axis, groups=None):
        return lax.all_to_all(
            part, axis, split_axis=0, concat_axis=0, axis_index_groups=groups, tiled=True
        )

    near, far = {}, {}
    for z in range(band_count):
        for p in range(owners):
            y, rest = divmod(p, 8)
            near.setdefault((z // 2, y // 2), []).append(z * owners + p)
            far.setdefault((z % 2, y % 2, rest), []).append(z * owners + p)
    near, far = list(near.values()), list(far.values())

    places = column_map.reshape(-1, 128)
    basis, send, small = kernel_call(
        pack_kernel,
        (
            shape(2 * rows, row_count),
            shape(slab, 8, 128),
            shape(3 * 8, row_count, dtype=jnp.int32),
        ),
        basis_re.reshape(-1, 128),
        basis_im.reshape(-1, 128),
        sphere_map,
        places,
        atom_sites,
        scratch=(
            pltpu.VMEM((2 * rows, 128), f32),
            pltpu.VMEM((2 * rows, 128), f32),
            pltpu.VMEM(sphere_map.shape, jnp.int32),
            pltpu.VMEM(places.shape, jnp.int32),
            pltpu.VMEM(atom_sites.shape, jnp.int32),
            pltpu.SemaphoreType.DMA((2, 4)),
            pltpu.SemaphoreType.DMA((3,)),
        ),
        far=(0, 1, 2, 3, 4),
        vmem=63,
    )
    psi = exchange(send, "band")

    phase_dims = (band_count, 2 * atoms, row_count)
    phase_sems = (pltpu.SemaphoreType.DMA((band_count,)),)
    phase_scratch = (pltpu.VMEM(phase_dims, bf16),) + phase_sems
    far_phase = kernel_call(
        lambda *refs: phase_kernel(grid, columns, *refs),
        shape(16 * band_count, *phase_dims[1:], dtype=bf16),
        small,
        scratch=phase_scratch,
        far_out=(0,),
        vmem=8,
        flops=10**7,
    )
    send, folded = kernel_call(
        lambda *refs: columns_kernel(columns, *refs),
        (shape(owners, planes, 128), shape(planes, 2 * half_x, 2 * half_y)),
        small,
        form_factors,
        far_phase,
        owner_table,
        potential,
        psi,
        scratch=phase_scratch
        + (pltpu.VMEM((band_count, 16, row_count), bf16),) * 2,
        far=(2,),
        grid=(2,),
    )
    got = exchange(send, "pw")
    send, phase = kernel_call(
        lambda *refs: planes_kernel(columns, grid, *refs),
        (shape(owners, planes, 128), shape(*phase_dims, dtype=bf16)),
        small,
        folded,
        table_x,
        table_y,
        far_phase,
        got,
        scratch=phase_sems
        + (
            pltpu.VMEM((2, 4 * planes, 8, row_count), f32),
            pltpu.VMEM((4, 8, row_count), f32),
            pltpu.VMEM((8, 2 * half_y, row_count), bf16),
            pltpu.VMEM((4 * planes * half_x, 2 * half_y), f32),
        ),
        grid=(3,),
        far=(4,),
        vmem=16,
    )
    got = exchange(send, "pw")
    send = kernel_call(
        lambda *refs: image_kernel(columns, waves, *refs),
        shape(band_count, 8, 128),
        small,
        form_factors,
        kinetic,
        channel_strength[None, :],
        phase,
        owner_table,
        psi,
        got,
    )
    got = exchange(send, "band")
    image, over, send = kernel_call(
        lambda *refs: products_kernel(waves, *refs),
        (
            shape(2 * slab, row_count),
            shape(2 * rows, 2 * rows),
            shape(len(near[0]), 1, 9 * 128),
        ),
        basis,
        got,
    )
    got = exchange(send, ("band", "pw"), near)
    send = kernel_call(gather_kernel, shape(len(far[0]), 1, 9 * 128), got)
    got = exchange(send, ("band", "pw"), far)
    next_re, next_im, coef_re, coef_im, chol_re, chol_im = kernel_call(
        finish_kernel,
        (
            shape(2 * slab, 128),
            shape(2 * slab, 128),
            shape(rows, slab),
            shape(rows, slab),
            shape(slab, slab),
            shape(slab, slab),
        ),
        basis,
        image,
        over,
        got,
    )
    return (
        next_re.reshape(slab, 1, row_count),
        next_im.reshape(slab, 1, row_count),
        coef_re.reshape(blocks, slab, slab),
        coef_im.reshape(blocks, slab, slab),
        chol_re,
        chol_im,
    )


def solution(mesh):
    return jax.shard_map(
        body,
        mesh=mesh,
        in_specs=(
            P(None, None, "band", "pw"),
            P(None, None, "band", "pw"),
            P("pw", None, None),
            P(None, "pw"),
            P(None, None, "pw"),
            P(),
            P(None, "pw"),
            P(),
            P(),
        ),
        out_specs=(P(None, "band", "pw"), P(None, "band", "pw"), P(), P(), P(), P()),
        check_vma=False,
    )
```

```python
import math

import jax
import jax.numpy as jnp
import numpy as np
from jax import lax
from jax.experimental import pallas as pl
from jax.experimental.pallas import tpu as pltpu
from jax.sharding import PartitionSpec as P

f32 = jnp.float32
bf16 = jnp.bfloat16
exact_mode = lax.Precision.HIGHEST

COS_POLY = (0.9999999403953552, -4.934792995452881, 4.058411121368408, -1.331876516342163, 0.21968960762023926)
SIN_POLY = (3.1415903568267822, -5.1674065589904785, 2.5440104007720947, -0.5594624280929565)
WHOLE = 1.5 * 2.0**23


def dot(left, right, left_dim=1, right_dim=0, precision=None):
    return lax.dot_general(
        left,
        right,
        (((left_dim,), (right_dim,)), ((), ())),
        precision=precision,
        preferred_element_type=f32,
    )


def split(part):
    high = part.astype(bf16)
    return high, (part - high.astype(f32)).astype(bf16)


def split3(part):
    high = part.astype(bf16)
    rest = part - high.astype(f32)
    middle = rest.astype(bf16)
    return [high, middle, (rest - middle.astype(f32)).astype(bf16)]


def dot3(left, right, left_dim=1, right_dim=0):
    lh, ll = left
    rh, rl = right
    return (
        dot(lh, rh, left_dim, right_dim)
        + dot(ll, rh, left_dim, right_dim)
        + dot(lh, rl, left_dim, right_dim)
    )


def pieces(table):
    table = table.astype(np.float32)
    high = table.astype(jnp.bfloat16)
    return [high, (table - high.astype(np.float32)).astype(jnp.bfloat16)]


def transform_tables(grid, planes, half_x, half_y):
    cos = np.array([math.cos(2.0 * math.pi * t / grid) for t in range(grid)])
    sin = np.array([math.sin(2.0 * math.pi * t / grid) for t in range(grid)])
    ticks = np.arange(grid)
    turns = ticks[:, None] * ticks[None, :] % grid
    order = ticks.reshape(grid // planes, planes).T.reshape(-1)
    by_owner = np.stack(pieces(cos[turns[order]]) + pieces(sin[turns[order]]))
    top = grid // 2 + 1

    def folded(half):
        table = np.zeros((2 * half, 2 * half))
        table[:top, :top] = cos[turns[:top, :top]]
        table[half + 1 : half + top - 1, half + 1 : half + top - 1] = sin[
            turns[1 : top - 1, 1 : top - 1]
        ]
        return pieces(table)

    high, low = folded(half_x)
    table_x = np.concatenate([high, low, high], 1)
    high, low = folded(half_y)
    table_y = np.concatenate([high, high, low], 0)
    return by_owner, table_x, table_y


def stripes(part, count):
    rows = part.shape[0] // count
    return jnp.concatenate([part[i * rows : (i + 1) * rows] for i in range(count)], 1)


def unstripe(part, count):
    width = part.shape[1] // count
    return jnp.concatenate([part[:, i * width : (i + 1) * width] for i in range(count)], 0)


def kernel_call(kernel, outs, *args, flops=10**6, vmem=8, scratch=(), far=(), far_out=(), grid=()):
    single = not isinstance(outs, tuple)
    outs = (outs,) if single else outs
    place = (pl.BlockSpec(memory_space=pltpu.VMEM), pl.BlockSpec(memory_space=pltpu.HBM))
    out = pl.pallas_call(
        kernel,
        out_shape=outs,
        in_specs=[place[i in far] for i in range(len(args))],
        scratch_shapes=scratch,
        grid=grid,
        out_specs=tuple(place[i in far_out] for i in range(len(outs))),
        compiler_params=pltpu.CompilerParams(vmem_limit_bytes=int(vmem * 2**20)),
        cost_estimate=pl.CostEstimate(flops=flops, bytes_accessed=4 * 10**6, transcendentals=0),
    )(*args)
    return out[0] if single else out


def shape(*dims, dtype=f32):
    return jax.ShapeDtypeStruct(dims, dtype)


def pack_kernel(
    far_re_ref,
    far_im_ref,
    far_map_ref,
    far_place_ref,
    far_sites_ref,
    basis_ref,
    send_ref,
    small_ref,
    re_ref,
    im_ref,
    map_ref,
    place_ref,
    sites_ref,
    sems,
    small_sems,
):
    count = sems.shape[1]
    small = [
        pltpu.make_async_copy(far, near, small_sems.at[i])
        for i, (far, near) in enumerate(
            ((far_map_ref, map_ref), (far_place_ref, place_ref), (far_sites_ref, sites_ref))
        )
    ]
    size = re_ref.shape[0] // count
    copies = [
        pltpu.make_async_copy(
            far.at[pl.ds(i * size, size)], near.at[pl.ds(i * size, size)], sems.at[part, i]
        )
        for part, (far, near) in enumerate(((far_re_ref, re_ref), (far_im_ref, im_ref)))
        for i in range(count)
    ]
    for copy in copies + small:
        copy.start()
    for copy in copies + small:
        copy.wait()
    count = map_ref.shape[0]
    lines = place_ref.shape[0] // 2
    small_ref[0:count, :] = map_ref[...]
    small_ref[count : count + lines, :] = jnp.concatenate(
        [place_ref[0:lines, :], place_ref[lines:, :]], 1
    )
    small_ref[count + lines :, :] = jnp.concatenate(
        [
            sites_ref[:, 0 : small_ref.shape[1]],
            sites_ref[:, small_ref.shape[1] :],
            jnp.zeros((2, small_ref.shape[1]), jnp.int32),
        ],
        0,
    )
    rows = re_ref.shape[0] // 2
    bands = send_ref.shape[0]

    def whole(ref):
        return jnp.concatenate(
            [ref[pl.ds(0, rows, stride=2), :], ref[pl.ds(1, rows, stride=2), :]], 1
        )

    basis = jnp.concatenate([whole(re_ref), whole(im_ref)], 0)
    basis_ref[...] = basis
    mixed = dot(basis, basis, 1, 1, exact_mode)
    over_re = mixed[:rows, :rows] + mixed[rows:, rows:]
    over_im = mixed[:rows, rows:] - mixed[rows:, :rows]
    line = lax.broadcasted_iota(jnp.int32, (rows, rows), 0)
    spot = lax.broadcasted_iota(jnp.int32, (rows, rows), 1)
    packed = stripes(jnp.where(line <= spot, over_re, over_im), 2)
    first = 2 * (rows - bands)
    for band in range(bands):
        send_ref[band, 0:2, :] = re_ref[first + 2 * band : first + 2 * band + 2, :]
        send_ref[band, 2:4, :] = im_ref[first + 2 * band : first + 2 * band + 2, :]
        send_ref[band, 4:8, :] = packed[4 * band : 4 * band + 4, :]


def phase_kernel(grid, columns, small_ref, far_ref, phase_ref, sems):
    groups, _, rows = phase_ref.shape
    atoms = phase_ref.shape[1] // 2
    copies = [
        pltpu.make_async_copy(phase_ref.at[s], far_ref.at[s], sems.at[s]) for s in range(groups)
    ]
    root = math.sqrt(2.0)
    cos_poly = [root * c / grid ** (2 * k) for k, c in enumerate(COS_POLY)]
    sin_poly = [root * c / grid ** (2 * k + 1) for k, c in enumerate(SIN_POLY)]
    sites = jnp.concatenate([small_ref[16:19, :], small_ref[19:22, :]], 1).astype(f32)
    sites = jnp.concatenate([sites, jnp.zeros((5, atoms), f32)], 0).astype(bf16)
    owner = lax.axis_index("pw")
    packs = rows // columns
    row = lax.div(owner, packs // 2)
    line = small_ref[pl.ds(groups + lax.rem(row, groups), 1), :]
    block = lax.div(row, groups) * (packs // 2) + lax.rem(owner, packs // 2)
    mine = jnp.zeros((1, columns), jnp.int32)
    for j in range(packs):
        chosen = (block == j).astype(jnp.int32)
        mine = mine + chosen * line[:, j * columns : (j + 1) * columns]
    mine = jnp.concatenate([mine, jnp.zeros((7, columns), jnp.int32)], 0).T[:, 0:1]
    column_x = lax.div(mine, grid).astype(f32)
    column_y = lax.rem(mine, grid).astype(f32)
    ticks = lax.broadcasted_iota(jnp.int32, (columns, rows), 0)
    for s in range(groups):
        cell = small_ref[s : s + 1, :]
        depth = lax.div(cell, columns).astype(f32)
        hot = ticks == lax.rem(cell, columns)
        x = jnp.sum(jnp.where(hot, column_x, 0.0), 0, keepdims=True)
        y = jnp.sum(jnp.where(hot, column_y, 0.0), 0, keepdims=True)
        place = jnp.concatenate([depth, x, y, jnp.zeros((5, rows), f32)], 0).astype(bf16)
        turns = dot(sites, place, 0, 0)
        turns = turns - grid * ((turns * (1.0 / grid) + WHOLE) - WHOLE)
        w = turns * turns
        c = cos_poly[-1]
        for value in cos_poly[-2::-1]:
            c = c * w + value
        h = sin_poly[-1]
        for value in sin_poly[-2::-1]:
            h = h * w + value
        h = h * turns
        phase_ref[s, 0:atoms, :] = (1.0 - h * h).astype(bf16)
        phase_ref[s, atoms : 2 * atoms, :] = (h * c).astype(bf16)
        copies[s].start()
    for copy in copies:
        copy.wait()


def two_rows(ref, s, line):
    return jnp.concatenate([ref[s, line : line + 1, :], ref[s, line + 1 : line + 2, :]], 1)


def make_copies(far_ref, near_ref, sems, first=0):
    return [
        pltpu.make_async_copy(far_ref.at[first + i], near_ref.at[i], sems.at[i])
        for i in range(near_ref.shape[0])
    ]


def fetch(far_ref, near_ref, sems, first=0):
    copies = make_copies(far_ref, near_ref, sems, first)
    for copy in copies:
        copy.start()
    return copies


def fold(pot_ref, out_ref):
    planes, grid, _ = pot_ref.shape

    def chooser(size):
        half = size // 2
        line = lax.broadcasted_iota(jnp.int32, (size, grid), 0)
        spot = lax.broadcasted_iota(jnp.int32, (size, grid), 1)
        t = jnp.where(line < half, line, line - half)
        plus = (line < half) & (t <= grid // 2) & (spot == t)
        minus = (line >= half) & (t > 0) & (t < grid // 2) & (spot == grid - t)
        return jnp.where(plus | minus, 1.0, 0.0).astype(bf16)

    lines = chooser(out_ref.shape[1])
    spots = chooser(out_ref.shape[2])
    for k in range(planes):
        part = sum(dot(lines, piece) for piece in split(pot_ref[k]))
        part = sum(dot(piece, spots, 1, 1) for piece in split(part))
        out_ref[k] = part * (1.0 / grid**3)


def columns_kernel(
    columns,
    small_ref,
    form_ref,
    far_ref,
    table_ref,
    pot_ref,
    got_ref,
    send_ref,
    fold_ref,
    phase_ref,
    sems,
    first_ref,
    second_ref,
):
    groups, _, rows = phase_ref.shape
    atoms = phase_ref.shape[1] // 2
    grid = table_ref.shape[1]
    owners, planes, _ = send_ref.shape
    channels = form_ref.shape[0]
    step = pl.program_id(0)

    @pl.when(step == 0)
    def to_depth():
        fetch(far_ref, phase_ref, sems)
        ticks = lax.broadcasted_iota(jnp.int32, (columns, rows), 0)
        deep = lax.broadcasted_iota(jnp.int32, (grid, rows), 0)
        total = jnp.zeros((4 * columns, grid), f32)
        for s in range(groups):
            psi_re = two_rows(got_ref, s, 0)
            psi_im = two_rows(got_ref, s, 2)
            cell = small_ref[s : s + 1, :]
            depth_hot = (deep == lax.div(cell, columns)).astype(f32).astype(bf16)
            hot = ticks == lax.rem(cell, columns)
            spread = jnp.concatenate(
                [jnp.where(hot, psi_re, 0.0), jnp.where(hot, psi_im, 0.0)], 0
            )
            total = total + dot(jnp.concatenate(split(spread), 0), depth_hot, 1, 1)
            form = form_ref[:, s, :]
            weighted_re = (form * psi_re).astype(bf16)
            weighted_im = (form * psi_im).astype(bf16)
            first_ref[s] = jnp.concatenate([weighted_re, weighted_im], 0)
            second_ref[s] = jnp.concatenate([-weighted_im, weighted_re], 0)
        column = split(total[: 2 * columns] + total[2 * columns :])
        by_cos = dot3((table_ref[0], table_ref[1]), column, 1, 1)
        by_sin = dot3((table_ref[2], table_ref[3]), column, 1, 1)
        deep_re = by_cos[:, :columns] - by_sin[:, columns:]
        deep_im = by_sin[:, :columns] + by_cos[:, columns:]
        for k in range(planes):
            lines = slice(owners * k, owners * (k + 1))
            send_ref[:, k, 0 : 2 * columns] = jnp.concatenate([deep_re[lines], deep_im[lines]], 1)

    @pl.when(step == 1)
    def space():
        fold(pot_ref, fold_ref)

    @pl.when(step == 2)
    def to_products():
        products = jnp.zeros((atoms, 2 * channels), f32)
        for copy in make_copies(far_ref, phase_ref, sems):
            copy.wait()
        for s in range(groups):
            products = products + (
                dot(phase_ref[s, 0:atoms, :], first_ref[s], 1, 1)
                + dot(phase_ref[s, atoms : 2 * atoms, :], second_ref[s], 1, 1)
            )
        parts = [products[owners * k : owners * (k + 1)] for k in range(atoms // owners)]
        half = len(parts) // 2
        overlap = jnp.sum(got_ref[:, 4:8, :], 0).T
        own = jnp.concatenate(
            [overlap[:owners], overlap[owners:], jnp.zeros((owners, 2 * columns - 8), f32)], 1
        )
        extra = [jnp.concatenate(parts[:half], 1), jnp.concatenate(parts[half:], 1), own]
        for k in range(planes):
            send_ref[:, k, 2 * columns :] = extra[k]


def planes_kernel(
    columns,
    grid,
    small_ref,
    fold_ref,
    table_x_ref,
    table_y_ref,
    far_ref,
    got_ref,
    send_ref,
    phase_ref,
    sems,
    value_ref,
    place_ref,
    hot_ref,
    field_ref,
):
    planes, size_x, size_y = fold_ref.shape
    half_x, half_y = size_x // 2, size_y // 2
    owners = got_ref.shape[0]
    steps, _, wide = phase_ref.shape
    lines, lanes = 2 * steps, wide // 2
    packs = lanes // columns
    ticks_x = lax.broadcasted_iota(jnp.int32, (half_x, wide), 0)
    ticks_y = lax.broadcasted_iota(jnp.int32, (half_y, wide), 0)
    count = 2 * planes

    def folded(at):
        t = jnp.minimum(at, grid - at)
        sign = jnp.where(at == t, 1.0, -1.0)
        return t.astype(f32), jnp.where((t == 0) | (2 * t == grid), 0.0, sign)

    def along_y(part):
        high, low = split(part)
        return dot(jnp.concatenate([high, low, high], 1), table_y_ref[...])

    def along_x(part):
        high, low = split(part)
        return dot(table_x_ref[...], jnp.concatenate([high, high, low], 0))

    def quarters(part):
        return (
            part[:half_x, :half_y],
            part[:half_x, half_y:],
            part[half_x:, :half_y],
            part[half_x:, half_y:],
        )

    def join(ee, eo, oe, oo):
        return jnp.concatenate(
            [jnp.concatenate([ee, eo], 1), jnp.concatenate([oe, oo], 1)], 0
        )

    step = pl.program_id(0)

    @pl.when(step == 0)
    def to_planes():
        fetch(far_ref, phase_ref, sems)
        place = small_ref[steps : 2 * steps, :]
        for i, at in enumerate((lax.div(place, grid), lax.rem(place, grid))):
            place_ref[2 * i], place_ref[2 * i + 1] = folded(at)
        for k in range(planes):
            loaded = [got_ref[pl.ds(j, lines, stride=packs), k, :] for j in range(packs)]
            for part in range(2):
                spot = slice(part * columns, (part + 1) * columns)
                value = jnp.concatenate([v[:, spot] for v in loaded], 1)
                value = jnp.concatenate([value[:steps], value[steps:]], 1)
                for piece, half in enumerate(split(value)):
                    half = half.astype(f32)
                    value_ref[piece, 2 * (2 * k + part)] = half
                    value_ref[piece, 2 * (2 * k + part) + 1] = half * place_ref[1]
        field = jnp.zeros((count * size_x, size_y), f32)
        for q in range(steps):
            hot_x = ticks_x == place_ref[0, q : q + 1, :].astype(jnp.int32)
            hot_y = ticks_y == place_ref[2, q : q + 1, :].astype(jnp.int32)
            hot_y = jnp.concatenate(
                [jnp.where(hot_y, 1.0, 0.0), jnp.where(hot_y, place_ref[3, q : q + 1, :], 0.0)], 0
            ).astype(bf16)
            hot_ref[q] = hot_y
            for piece in range(2):
                spread = [
                    jnp.where(hot_x, value_ref[piece, i, q : q + 1, :], 0.0) for i in range(2 * count)
                ]
                field = field + dot(jnp.concatenate(spread, 0).astype(bf16), hot_y, 1, 1)
        field_ref[...] = field

    @pl.when(step == 1)
    def transforms():
        field = along_y(field_ref[...])
        back = []
        for k in range(planes):
            re, im = [
                quarters(along_x(field[(2 * k + i) * size_x : (2 * k + i + 1) * size_x]))
                for i in range(2)
            ]
            values_v = quarters(fold_ref[k])
            real_sum, real_gap = re[0] - re[3], re[0] + re[3]
            imag_sum, imag_gap = im[0] - im[3], im[0] + im[3]
            cross_re, cross_re_gap = re[1] + re[2], re[1] - re[2]
            cross_im, cross_im_gap = im[1] + im[2], im[1] - im[2]
            pp_re, mm_re = real_sum - cross_im, real_sum + cross_im
            pp_im, mm_im = imag_sum + cross_re, imag_sum - cross_re
            pm_re, mp_re = real_gap + cross_im_gap, real_gap - cross_im_gap
            pm_im, mp_im = imag_gap - cross_re_gap, imag_gap + cross_re_gap
            parts = []
            for pp, pm, mp, mm in (
                (pp_re, pm_re, mp_re, mm_re),
                (pp_im, pm_im, mp_im, mm_im),
            ):
                pp, pm, mp, mm = [a * b for a, b in zip((pp, pm, mp, mm), values_v)]
                plus_s, plus_g = pp + pm, pp - pm
                minus_s, minus_g = mp + mm, mp - mm
                parts.append((plus_s + minus_s, plus_g + minus_g, plus_s - minus_s, plus_g - minus_g))
            re, im = parts
            back.append(along_x(join(re[0], im[1], im[2], -re[3])))
            back.append(along_x(join(im[0], -re[1], -re[2], -im[3])))
        field_ref[...] = along_y(jnp.concatenate(back, 0))

    @pl.when(step == 2)
    def to_columns():
        high, low = split(field_ref[...])
        for q in range(steps):
            hot_x = ticks_x == place_ref[0, q : q + 1, :].astype(jnp.int32)
            sign_x = place_ref[1, q : q + 1, :]
            hot_y = hot_ref[q]
            mixed = dot(high, hot_y) + dot(low, hot_y)
            for i in range(count):
                even = mixed[i * size_x : i * size_x + half_x]
                odd = mixed[i * size_x + half_x : (i + 1) * size_x]
                picked = jnp.where(hot_x, even + sign_x * odd, 0.0)
                value_ref[0, i, q : q + 1, :] = jnp.sum(picked, 0, keepdims=True)
        for k in range(planes):
            halves = [value_ref[0, 2 * k + i] for i in range(2)]
            halves = [jnp.concatenate([v[:, :lanes], v[:, lanes:]], 0) for v in halves]
            ride = jnp.sum(got_ref[:, k, 2 * columns :], 0, keepdims=True)
            ride = jnp.broadcast_to(ride, (lines, ride.shape[1]))
            for j in range(packs):
                spot = slice(j * columns, (j + 1) * columns)
                send_ref[pl.ds(j, lines, stride=packs), k, :] = jnp.concatenate(
                    [halves[0][:, spot], halves[1][:, spot], ride], 1
                )
        for copy in make_copies(far_ref, phase_ref, sems):
            copy.wait()


def image_kernel(
    columns,
    waves,
    small_ref,
    form_ref,
    kinetic_ref,
    strength_ref,
    phase_ref,
    table_ref,
    psi_ref,
    got_ref,
    send_ref,
):
    groups, _, rows = phase_ref.shape
    atoms = phase_ref.shape[1] // 2
    grid = table_ref.shape[1]
    owners, planes, _ = got_ref.shape
    channels = form_ref.shape[0]
    root = math.sqrt(waves)
    got = [got_ref[:, k, :] for k in range(planes)]
    ride = [g[:, 2 * columns :] for g in got]
    wide = 2 * channels
    per_row = 2 * columns // wide
    sums = jnp.concatenate(
        [r[:, wide * i : wide * (i + 1)] for r in ride[:2] for i in range(per_row)], 0
    ).T
    line = lax.broadcasted_iota(jnp.int32, (wide, channels), 0)
    spot = lax.broadcasted_iota(jnp.int32, (wide, channels), 1)
    factor = jnp.sum(
        jnp.where(lax.rem(line, channels) == spot, strength_ref[...], 0.0), 1, keepdims=True
    )
    scaled = factor * (sums / root) / root
    scaled_re = scaled[:channels].astype(bf16)
    scaled_im = scaled[channels:].astype(bf16)
    first = jnp.concatenate([scaled_re, scaled_im], 0)
    second = jnp.concatenate([scaled_im, -scaled_re], 0)
    deep = split(jnp.concatenate([g[:, : 2 * columns] for g in got], 0).T)
    by_cos = dot3(deep, (table_ref[0], table_ref[1]))
    by_sin = dot3(deep, (table_ref[2], table_ref[3]))
    out_re = by_cos[:columns] + by_sin[columns:]
    out_im = by_cos[columns:] - by_sin[:columns]
    out = jnp.concatenate(split(jnp.concatenate([out_re, out_im], 0)), 0)
    ticks = lax.broadcasted_iota(jnp.int32, (columns, rows), 0)
    depths = lax.broadcasted_iota(jnp.int32, (grid, rows), 0)
    overlap = jnp.concatenate([ride[2][:, 0:4].T, ride[2][:, 4:8].T], 1)
    for s in range(groups):
        cell = small_ref[s : s + 1, :]
        depth_hot = (depths == lax.div(cell, columns)).astype(f32).astype(bf16)
        hot = ticks == lax.rem(cell, columns)
        found = dot(out, depth_hot)
        found = found[: 2 * columns] + found[2 * columns :]
        local_re = jnp.sum(jnp.where(hot, found[:columns], 0.0), 0, keepdims=True)
        local_im = jnp.sum(jnp.where(hot, found[columns:], 0.0), 0, keepdims=True)
        form = form_ref[:, s, :]
        mixed = dot(first, phase_ref[s, 0:atoms, :]) + dot(
            second, phase_ref[s, atoms : 2 * atoms, :]
        )
        near_re = jnp.sum(form * mixed[:channels], 0, keepdims=True)
        near_im = jnp.sum(form * mixed[channels:], 0, keepdims=True)
        kinetic = kinetic_ref[s : s + 1, :]
        image_re = kinetic * two_rows(psi_ref, s, 0) + local_re + near_re
        image_im = kinetic * two_rows(psi_ref, s, 2) + local_im + near_im
        send_ref[s, 0:1, :] = image_re[:, :128]
        send_ref[s, 1:2, :] = image_re[:, 128:]
        send_ref[s, 2:3, :] = image_im[:, :128]
        send_ref[s, 3:4, :] = image_im[:, 128:]
        send_ref[s, 4:8, :] = overlap


def overlap(waves, got_ref, over_ref):
    size = over_ref.shape[0] // 2
    packed = jnp.concatenate([got_ref[d, 4:8, :] for d in range(got_ref.shape[0])], 0)
    packed = unstripe(packed, 2) * (1.0 / waves)
    line = lax.broadcasted_iota(jnp.int32, (size, size), 0)
    spot = lax.broadcasted_iota(jnp.int32, (size, size), 1)
    turned = packed.T
    over_re = jnp.where(line <= spot, packed, turned)
    over_im = jnp.where(line < spot, -turned, jnp.where(line > spot, packed, 0.0))
    over_ref[...] = jnp.concatenate(
        [jnp.concatenate([over_re, -over_im], 1), jnp.concatenate([over_im, over_re], 1)], 0
    )


def products_kernel(waves, basis_ref, got_ref, image_ref, over_ref, send_ref):
    overlap(waves, got_ref, over_ref)
    bands = got_ref.shape[0]
    half = basis_ref.shape[0] // 2
    owners = send_ref.shape[0]
    image_re = jnp.concatenate([got_ref[:, 0, :], got_ref[:, 1, :]], 1)
    image_im = jnp.concatenate([got_ref[:, 2, :], got_ref[:, 3, :]], 1)
    image = jnp.concatenate([image_re, image_im], 0)
    image_ref[...] = image
    mixed = dot(image, basis_ref[...], 1, 1, exact_mode) * (1.0 / waves)
    coef_re = mixed[:bands, :half] + mixed[bands:, half:]
    coef_im = mixed[bands:, :half] - mixed[:bands, half:]
    coef = jnp.concatenate([coef_re, coef_im], 1)
    own = dot(image, image, 1, 1, exact_mode) * (1.0 / waves)
    own_re = own[:bands, :bands] + own[bands:, bands:]
    own_im = own[:bands, bands:] - own[bands:, :bands]
    line = lax.broadcasted_iota(jnp.int32, (bands, bands), 0)
    spot = lax.broadcasted_iota(jnp.int32, (bands, bands), 1)
    packed = jnp.where(line <= spot, own_re, own_im)
    row = jnp.concatenate(
        [stripes(coef, bands), stripes(packed, bands), jnp.zeros((1, 128 - bands * bands), f32)], 1
    )
    send_ref[:, 0, :] = jnp.broadcast_to(row, (owners, row.shape[1]))


def gather_kernel(got_ref, send_ref):
    row = jnp.sum(got_ref[:, 0, :], 0, keepdims=True)
    send_ref[:, 0, :] = jnp.broadcast_to(row, (send_ref.shape[0], row.shape[1]))


def finish_kernel(
    basis_ref, image_ref, over_ref, got_ref, next_re_ref, next_im_ref, coef_re_ref, coef_im_ref, chol_re_ref, chol_im_ref
):
    bands = image_ref.shape[0] // 2
    half = basis_ref.shape[0] // 2
    row = jnp.sum(got_ref[:, 0, :], 0, keepdims=True)
    size = bands * 2 * half
    coef = unstripe(row[:, :size], bands)
    packed = unstripe(row[:, size : size + bands * bands], bands)
    coef_re = coef[:, :half]
    coef_im = coef[:, half:]
    coef_re_ref[...] = coef_re.T
    coef_im_ref[...] = coef_im.T
    line = lax.broadcasted_iota(jnp.int32, (bands, bands), 0)
    spot = lax.broadcasted_iota(jnp.int32, (bands, bands), 1)
    turned = packed.T
    own_re = jnp.where(line <= spot, packed, turned)
    own_im = jnp.where(line < spot, -turned, jnp.where(line > spot, packed, 0.0))
    left = dot(coef, over_ref[...], 1, 0, exact_mode) - 2.0 * coef
    stacked = jnp.concatenate([coef, jnp.concatenate([-coef_im, coef_re], 1)], 0)
    mixed = dot(stacked, left, 1, 1, exact_mode)
    gram_re = own_re + mixed[:bands]
    gram_im = own_im + mixed[bands:]
    eye = jnp.where(line == spot, 1.0, 0.0)
    work_re = jnp.concatenate([gram_re, eye], 1)
    work_im = jnp.concatenate([gram_im, jnp.zeros_like(eye)], 1)
    rows_re, rows_im = [], []
    for k in range(bands):
        pivot = lax.rsqrt(work_re[k : k + 1, k : k + 1])
        lead_re = work_re[k : k + 1, :] * pivot
        lead_im = work_im[k : k + 1, :] * pivot
        rows_re.append(lead_re)
        rows_im.append(lead_im)
        if k + 1 < bands:
            column_re = work_re[:, k : k + 1] * pivot
            column_im = work_im[:, k : k + 1] * pivot
            work_re, work_im = (
                work_re - (column_re * lead_re - column_im * lead_im),
                work_im - (column_re * lead_im + column_im * lead_re),
            )
    all_re = jnp.concatenate(rows_re, 0)
    all_im = jnp.concatenate(rows_im, 0)
    chol_re_ref[...] = jnp.where(line <= spot, all_re[:, :bands], 0.0)
    chol_im_ref[...] = jnp.where(line < spot, all_im[:, :bands], 0.0)
    inv_re = all_re[:, bands:]
    inv_im = all_im[:, bands:]
    basis_re = basis_ref[0:half, :]
    basis_im = basis_ref[half : 2 * half, :]
    span_re = dot(coef, jnp.concatenate([basis_re, -basis_im], 0), 1, 0, exact_mode)
    span_im = dot(coef, jnp.concatenate([basis_im, basis_re], 0), 1, 0, exact_mode)
    rest_re = image_ref[0:bands, :] - span_re
    rest_im = image_ref[bands : 2 * bands, :] - span_im
    next_re = dot(inv_re, rest_re, 1, 0, exact_mode) + dot(inv_im, rest_im, 1, 0, exact_mode)
    next_im = dot(inv_re, rest_im, 1, 0, exact_mode) - dot(inv_im, rest_re, 1, 0, exact_mode)
    for ref, value in ((next_re_ref, next_re), (next_im_ref, next_im)):
        ref[pl.ds(0, bands, stride=2), :] = value[:, :128]
        ref[pl.ds(1, bands, stride=2), :] = value[:, 128:]


def body(
    basis_re,
    basis_im,
    potential,
    kinetic,
    form_factors,
    channel_strength,
    sphere_map,
    column_map,
    atom_sites,
):
    blocks, slab, _, row_count = basis_re.shape
    band_count = lax.axis_size("band")
    owners = lax.axis_size("pw")
    planes, grid, _ = potential.shape
    columns = column_map.shape[0] // owners
    waves = band_count * owners * row_count
    atoms = atom_sites.shape[1]
    rows = blocks * slab
    half_x, half_y = grid // 2 + 8, 128
    tables = transform_tables(grid, planes, half_x, half_y)
    owner_table, table_x, table_y = [jnp.asarray(table) for table in tables]

    def exchange(part, axis, groups=None):
        return lax.all_to_all(
            part, axis, split_axis=0, concat_axis=0, axis_index_groups=groups, tiled=True
        )

    near, far = {}, {}
    for z in range(band_count):
        for p in range(owners):
            y, rest = divmod(p, 8)
            near.setdefault((z // 2, y), []).append(z * owners + p)
            far.setdefault((z % 2, rest), []).append(z * owners + p)
    near, far = list(near.values()), list(far.values())

    places = column_map.reshape(-1, 128)
    basis, send, small = kernel_call(
        pack_kernel,
        (
            shape(2 * rows, row_count),
            shape(slab, 8, 128),
            shape(3 * 8, row_count, dtype=jnp.int32),
        ),
        basis_re.reshape(-1, 128),
        basis_im.reshape(-1, 128),
        sphere_map,
        places,
        atom_sites,
        scratch=(
            pltpu.VMEM((2 * rows, 128), f32),
            pltpu.VMEM((2 * rows, 128), f32),
            pltpu.VMEM(sphere_map.shape, jnp.int32),
            pltpu.VMEM(places.shape, jnp.int32),
            pltpu.VMEM(atom_sites.shape, jnp.int32),
            pltpu.SemaphoreType.DMA((2, 4)),
            pltpu.SemaphoreType.DMA((3,)),
        ),
        far=(0, 1, 2, 3, 4),
        vmem=63,
    )
    psi = exchange(send, "band")

    phase_dims = (band_count, 2 * atoms, row_count)
    phase_sems = (pltpu.SemaphoreType.DMA((band_count,)),)
    phase_scratch = (pltpu.VMEM(phase_dims, bf16),) + phase_sems
    far_phase = kernel_call(
        lambda *refs: phase_kernel(grid, columns, *refs),
        shape(16 * band_count, *phase_dims[1:], dtype=bf16),
        small,
        scratch=phase_scratch,
        far_out=(0,),
        vmem=8,
        flops=10**7,
    )
    send, folded = kernel_call(
        lambda *refs: columns_kernel(columns, *refs),
        (shape(owners, planes, 128), shape(planes, 2 * half_x, 2 * half_y)),
        small,
        form_factors,
        far_phase,
        owner_table,
        potential,
        psi,
        scratch=phase_scratch
        + (pltpu.VMEM((band_count, 16, row_count), bf16),) * 2,
        far=(2,),
        grid=(3,),
    )
    got = exchange(send, "pw")
    send, phase = kernel_call(
        lambda *refs: planes_kernel(columns, grid, *refs),
        (shape(owners, planes, 128), shape(*phase_dims, dtype=bf16)),
        small,
        folded,
        table_x,
        table_y,
        far_phase,
        got,
        scratch=phase_sems
        + (
            pltpu.VMEM((2, 4 * planes, 8, row_count), f32),
            pltpu.VMEM((4, 8, row_count), f32),
            pltpu.VMEM((8, 2 * half_y, row_count), bf16),
            pltpu.VMEM((4 * planes * half_x, 2 * half_y), f32),
        ),
        grid=(3,),
        far=(4,),
        vmem=16,
    )
    got = exchange(send, "pw")
    send = kernel_call(
        lambda *refs: image_kernel(columns, waves, *refs),
        shape(band_count, 8, 128),
        small,
        form_factors,
        kinetic,
        channel_strength[None, :],
        phase,
        owner_table,
        psi,
        got,
    )
    got = exchange(send, "band")
    image, over, send = kernel_call(
        lambda *refs: products_kernel(waves, *refs),
        (
            shape(2 * slab, row_count),
            shape(2 * rows, 2 * rows),
            shape(len(near[0]), 1, 9 * 128),
        ),
        basis,
        got,
    )
    got = exchange(send, ("band", "pw"), near)
    send = kernel_call(gather_kernel, shape(len(far[0]), 1, 9 * 128), got)
    got = exchange(send, ("band", "pw"), far)
    next_re, next_im, coef_re, coef_im, chol_re, chol_im = kernel_call(
        finish_kernel,
        (
            shape(2 * slab, 128),
            shape(2 * slab, 128),
            shape(rows, slab),
            shape(rows, slab),
            shape(slab, slab),
            shape(slab, slab),
        ),
        basis,
        image,
        over,
        got,
    )
    return (
        next_re.reshape(slab, 1, row_count),
        next_im.reshape(slab, 1, row_count),
        coef_re.reshape(blocks, slab, slab),
        coef_im.reshape(blocks, slab, slab),
        chol_re,
        chol_im,
    )


def solution(mesh):
    return jax.shard_map(
        body,
        mesh=mesh,
        in_specs=(
            P(None, None, "band", "pw"),
            P(None, None, "band", "pw"),
            P("pw", None, None),
            P(None, "pw"),
            P(None, None, "pw"),
            P(),
            P(None, "pw"),
            P(),
            P(),
        ),
        out_specs=(P(None, "band", "pw"), P(None, "band", "pw"), P(), P(), P(), P()),
        check_vma=False,
    )
```

```python
import math

import jax
import jax.numpy as jnp
import numpy as np
from jax import lax
from jax.experimental import pallas as pl
from jax.experimental.pallas import tpu as pltpu
from jax.sharding import PartitionSpec as P

f32 = jnp.float32
bf16 = jnp.bfloat16
exact_mode = lax.Precision.HIGHEST

COS_POLY = (0.9999999403953552, -4.934792995452881, 4.058411121368408, -1.331876516342163, 0.21968960762023926)
SIN_POLY = (3.1415903568267822, -5.1674065589904785, 2.5440104007720947, -0.5594624280929565)
WHOLE = 1.5 * 2.0**23


def dot(left, right, left_dim=1, right_dim=0, precision=None):
    return lax.dot_general(
        left,
        right,
        (((left_dim,), (right_dim,)), ((), ())),
        precision=precision,
        preferred_element_type=f32,
    )


def split(part):
    high = part.astype(bf16)
    return high, (part - high.astype(f32)).astype(bf16)


def split3(part):
    high = part.astype(bf16)
    rest = part - high.astype(f32)
    middle = rest.astype(bf16)
    return [high, middle, (rest - middle.astype(f32)).astype(bf16)]


def dot3(left, right, left_dim=1, right_dim=0):
    lh, ll = left
    rh, rl = right
    return (
        dot(lh, rh, left_dim, right_dim)
        + dot(ll, rh, left_dim, right_dim)
        + dot(lh, rl, left_dim, right_dim)
    )


def pieces(table):
    table = table.astype(np.float32)
    high = table.astype(jnp.bfloat16)
    return [high, (table - high.astype(np.float32)).astype(jnp.bfloat16)]


def transform_tables(grid, planes, half_x, half_y):
    cos = np.array([math.cos(2.0 * math.pi * t / grid) for t in range(grid)])
    sin = np.array([math.sin(2.0 * math.pi * t / grid) for t in range(grid)])
    ticks = np.arange(grid)
    turns = ticks[:, None] * ticks[None, :] % grid
    order = ticks.reshape(grid // planes, planes).T.reshape(-1)
    by_owner = np.stack(pieces(cos[turns[order]]) + pieces(sin[turns[order]]))
    top = grid // 2 + 1

    def folded(half):
        table = np.zeros((2 * half, 2 * half))
        table[:top, :top] = cos[turns[:top, :top]]
        table[half + 1 : half + top - 1, half + 1 : half + top - 1] = sin[
            turns[1 : top - 1, 1 : top - 1]
        ]
        return pieces(table)

    high, low = folded(half_x)
    table_x = np.concatenate([high, low, high], 1)
    high, low = folded(half_y)
    table_y = np.concatenate([high, high, low], 0)
    return by_owner, table_x, table_y


def stripes(part, count):
    rows = part.shape[0] // count
    return jnp.concatenate([part[i * rows : (i + 1) * rows] for i in range(count)], 1)


def unstripe(part, count):
    width = part.shape[1] // count
    return jnp.concatenate([part[:, i * width : (i + 1) * width] for i in range(count)], 0)


def kernel_call(kernel, outs, *args, flops=10**6, vmem=8, scratch=(), far=(), far_out=(), grid=(), aliases=None):
    single = not isinstance(outs, tuple)
    outs = (outs,) if single else outs
    place = (pl.BlockSpec(memory_space=pltpu.VMEM), pl.BlockSpec(memory_space=pltpu.HBM))
    out = pl.pallas_call(
        kernel,
        out_shape=outs,
        in_specs=[place[i in far] for i in range(len(args))],
        scratch_shapes=scratch,
        grid=grid,
        input_output_aliases=aliases or {},
        out_specs=tuple(place[i in far_out] for i in range(len(outs))),
        compiler_params=pltpu.CompilerParams(vmem_limit_bytes=int(vmem * 2**20)),
        cost_estimate=pl.CostEstimate(flops=flops, bytes_accessed=4 * 10**6, transcendentals=0),
    )(*args)
    return out[0] if single else out


def shape(*dims, dtype=f32):
    return jax.ShapeDtypeStruct(dims, dtype)


def pack_kernel(
    far_re_ref,
    far_im_ref,
    far_map_ref,
    far_place_ref,
    far_sites_ref,
    basis_ref,
    send_ref,
    small_ref,
    re_ref,
    im_ref,
    map_ref,
    place_ref,
    sites_ref,
    sems,
    small_sems,
):
    count = sems.shape[1]
    small = [
        pltpu.make_async_copy(far, near, small_sems.at[i])
        for i, (far, near) in enumerate(
            ((far_map_ref, map_ref), (far_place_ref, place_ref), (far_sites_ref, sites_ref))
        )
    ]
    size = re_ref.shape[0] // count
    copies = [
        pltpu.make_async_copy(
            far.at[pl.ds(i * size, size)], near.at[pl.ds(i * size, size)], sems.at[part, i]
        )
        for part, (far, near) in enumerate(((far_re_ref, re_ref), (far_im_ref, im_ref)))
        for i in range(count)
    ]
    for copy in copies + small:
        copy.start()
    for copy in copies + small:
        copy.wait()
    count = map_ref.shape[0]
    lines = place_ref.shape[0] // 2
    small_ref[0:count, :] = map_ref[...]
    small_ref[count : count + lines, :] = jnp.concatenate(
        [place_ref[0:lines, :], place_ref[lines:, :]], 1
    )
    small_ref[count + lines :, :] = jnp.concatenate(
        [
            sites_ref[:, 0 : small_ref.shape[1]],
            sites_ref[:, small_ref.shape[1] :],
            jnp.zeros((2, small_ref.shape[1]), jnp.int32),
        ],
        0,
    )
    rows = re_ref.shape[0] // 2
    bands = send_ref.shape[0]

    def whole(ref):
        return jnp.concatenate(
            [ref[pl.ds(0, rows, stride=2), :], ref[pl.ds(1, rows, stride=2), :]], 1
        )

    basis = jnp.concatenate([whole(re_ref), whole(im_ref)], 0)
    basis_ref[...] = basis
    mixed = dot(basis, basis, 1, 1, exact_mode)
    over_re = mixed[:rows, :rows] + mixed[rows:, rows:]
    over_im = mixed[:rows, rows:] - mixed[rows:, :rows]
    line = lax.broadcasted_iota(jnp.int32, (rows, rows), 0)
    spot = lax.broadcasted_iota(jnp.int32, (rows, rows), 1)
    packed = stripes(jnp.where(line <= spot, over_re, over_im), 2)
    first = 2 * (rows - bands)
    for band in range(bands):
        send_ref[band, 0:2, :] = re_ref[first + 2 * band : first + 2 * band + 2, :]
        send_ref[band, 2:4, :] = im_ref[first + 2 * band : first + 2 * band + 2, :]
        send_ref[band, 4:8, :] = packed[4 * band : 4 * band + 4, :]


def phase_blocks(grid, columns, small_ref, phase_ref, blocks):
    groups, _, rows = phase_ref.shape
    atoms = phase_ref.shape[1] // 2
    root = math.sqrt(2.0)
    cos_poly = [root * c / grid ** (2 * k) for k, c in enumerate(COS_POLY)]
    sin_poly = [root * c / grid ** (2 * k + 1) for k, c in enumerate(SIN_POLY)]
    sites = jnp.concatenate([small_ref[16:19, :], small_ref[19:22, :]], 1).astype(f32)
    sites = jnp.concatenate([sites, jnp.zeros((5, atoms), f32)], 0).astype(bf16)
    owner = lax.axis_index("pw")
    packs = rows // columns
    row = lax.div(owner, packs // 2)
    line = small_ref[pl.ds(groups + lax.rem(row, groups), 1), :]
    block = lax.div(row, groups) * (packs // 2) + lax.rem(owner, packs // 2)
    mine = jnp.zeros((1, columns), jnp.int32)
    for j in range(packs):
        chosen = (block == j).astype(jnp.int32)
        mine = mine + chosen * line[:, j * columns : (j + 1) * columns]
    mine = jnp.concatenate([mine, jnp.zeros((7, columns), jnp.int32)], 0).T[:, 0:1]
    column_x = lax.div(mine, grid).astype(f32)
    column_y = lax.rem(mine, grid).astype(f32)
    ticks = lax.broadcasted_iota(jnp.int32, (columns, rows), 0)
    for s in blocks:
        cell = small_ref[s : s + 1, :]
        depth = lax.div(cell, columns).astype(f32)
        hot = ticks == lax.rem(cell, columns)
        x = jnp.sum(jnp.where(hot, column_x, 0.0), 0, keepdims=True)
        y = jnp.sum(jnp.where(hot, column_y, 0.0), 0, keepdims=True)
        place = jnp.concatenate([depth, x, y, jnp.zeros((5, rows), f32)], 0).astype(bf16)
        turns = dot(sites, place, 0, 0)
        turns = turns - grid * ((turns * (1.0 / grid) + WHOLE) - WHOLE)
        w = turns * turns
        c = cos_poly[-1]
        for value in cos_poly[-2::-1]:
            c = c * w + value
        h = sin_poly[-1]
        for value in sin_poly[-2::-1]:
            h = h * w + value
        h = h * turns
        phase_ref[s, 0:atoms, :] = (1.0 - h * h).astype(bf16)
        phase_ref[s, atoms : 2 * atoms, :] = (h * c).astype(bf16)
        yield s


def phase_kernel(grid, columns, first, small_ref, far_ref, phase_ref, sems):
    copies = [
        pltpu.make_async_copy(phase_ref.at[s], far_ref.at[s], sems.at[s]) for s in range(first)
    ]
    for s in phase_blocks(grid, columns, small_ref, phase_ref, range(first)):
        copies[s].start()
    for copy in copies:
        copy.wait()


def two_rows(ref, s, line):
    return jnp.concatenate([ref[s, line : line + 1, :], ref[s, line + 1 : line + 2, :]], 1)


def make_copies(far_ref, near_ref, sems, first=0):
    return [
        pltpu.make_async_copy(far_ref.at[first + i], near_ref.at[i], sems.at[i])
        for i in range(near_ref.shape[0])
    ]


def fetch(far_ref, near_ref, sems, first=0):
    copies = make_copies(far_ref, near_ref, sems, first)
    for copy in copies:
        copy.start()
    return copies


def fold(pot_ref, out_ref):
    planes, grid, _ = pot_ref.shape

    def chooser(size):
        half = size // 2
        line = lax.broadcasted_iota(jnp.int32, (size, grid), 0)
        spot = lax.broadcasted_iota(jnp.int32, (size, grid), 1)
        t = jnp.where(line < half, line, line - half)
        plus = (line < half) & (t <= grid // 2) & (spot == t)
        minus = (line >= half) & (t > 0) & (t < grid // 2) & (spot == grid - t)
        return jnp.where(plus | minus, 1.0, 0.0).astype(bf16)

    lines = chooser(out_ref.shape[1])
    spots = chooser(out_ref.shape[2])
    for k in range(planes):
        part = sum(dot(lines, piece) for piece in split(pot_ref[k]))
        part = sum(dot(piece, spots, 1, 1) for piece in split(part))
        out_ref[k] = part * (1.0 / grid**3)


def columns_kernel(
    columns,
    first,
    small_ref,
    form_ref,
    _,
    table_ref,
    pot_ref,
    got_ref,
    send_ref,
    fold_ref,
    far_ref,
    phase_ref,
    sems,
    first_ref,
    second_ref,
):
    groups, _, rows = phase_ref.shape
    atoms = phase_ref.shape[1] // 2
    grid = table_ref.shape[1]
    owners, planes, _ = send_ref.shape
    channels = form_ref.shape[0]
    step = pl.program_id(0)
    copies = []
    for s in range(groups):
        ends = (far_ref.at[s], phase_ref.at[s])
        copies.append(pltpu.make_async_copy(*(ends if s < first else ends[::-1]), sems.at[s]))

    @pl.when(step == 0)
    def to_depth():
        for copy in copies[:first]:
            copy.start()
        ticks = lax.broadcasted_iota(jnp.int32, (columns, rows), 0)
        deep = lax.broadcasted_iota(jnp.int32, (grid, rows), 0)
        total = jnp.zeros((4 * columns, grid), f32)
        for s in range(groups):
            psi_re = two_rows(got_ref, s, 0)
            psi_im = two_rows(got_ref, s, 2)
            cell = small_ref[s : s + 1, :]
            depth_hot = (deep == lax.div(cell, columns)).astype(f32).astype(bf16)
            hot = ticks == lax.rem(cell, columns)
            spread = jnp.concatenate(
                [jnp.where(hot, psi_re, 0.0), jnp.where(hot, psi_im, 0.0)], 0
            )
            total = total + dot(jnp.concatenate(split(spread), 0), depth_hot, 1, 1)
            form = form_ref[:, s, :]
            weighted_re = (form * psi_re).astype(bf16)
            weighted_im = (form * psi_im).astype(bf16)
            first_ref[s] = jnp.concatenate([weighted_re, weighted_im], 0)
            second_ref[s] = jnp.concatenate([-weighted_im, weighted_re], 0)
        column = split(total[: 2 * columns] + total[2 * columns :])
        by_cos = dot3((table_ref[0], table_ref[1]), column, 1, 1)
        by_sin = dot3((table_ref[2], table_ref[3]), column, 1, 1)
        deep_re = by_cos[:, :columns] - by_sin[:, columns:]
        deep_im = by_sin[:, :columns] + by_cos[:, columns:]
        for k in range(planes):
            lines = slice(owners * k, owners * (k + 1))
            send_ref[:, k, 0 : 2 * columns] = jnp.concatenate([deep_re[lines], deep_im[lines]], 1)

    @pl.when(step == 1)
    def space():
        fold(pot_ref, fold_ref)
        for s in phase_blocks(grid, columns, small_ref, phase_ref, range(first, groups)):
            copies[s].start()

    @pl.when(step == 2)
    def to_products():
        products = jnp.zeros((atoms, 2 * channels), f32)
        for copy in copies[:first]:
            copy.wait()
        for s in range(groups):
            products = products + (
                dot(phase_ref[s, 0:atoms, :], first_ref[s], 1, 1)
                + dot(phase_ref[s, atoms : 2 * atoms, :], second_ref[s], 1, 1)
            )
        parts = [products[owners * k : owners * (k + 1)] for k in range(atoms // owners)]
        half = len(parts) // 2
        overlap = jnp.sum(got_ref[:, 4:8, :], 0).T
        own = jnp.concatenate(
            [overlap[:owners], overlap[owners:], jnp.zeros((owners, 2 * columns - 8), f32)], 1
        )
        extra = [jnp.concatenate(parts[:half], 1), jnp.concatenate(parts[half:], 1), own]
        for k in range(planes):
            send_ref[:, k, 2 * columns :] = extra[k]
        for copy in copies[first:]:
            copy.wait()


def planes_kernel(
    columns,
    grid,
    small_ref,
    fold_ref,
    table_x_ref,
    table_y_ref,
    far_ref,
    got_ref,
    send_ref,
    phase_ref,
    sems,
    value_ref,
    place_ref,
    hot_ref,
    field_ref,
):
    planes, size_x, size_y = fold_ref.shape
    half_x, half_y = size_x // 2, size_y // 2
    owners = got_ref.shape[0]
    steps, _, wide = phase_ref.shape
    lines, lanes = 2 * steps, wide // 2
    packs = lanes // columns
    ticks_x = lax.broadcasted_iota(jnp.int32, (half_x, wide), 0)
    ticks_y = lax.broadcasted_iota(jnp.int32, (half_y, wide), 0)
    count = 2 * planes

    def folded(at):
        t = jnp.minimum(at, grid - at)
        sign = jnp.where(at == t, 1.0, -1.0)
        return t.astype(f32), jnp.where((t == 0) | (2 * t == grid), 0.0, sign)

    def along_y(part):
        high, low = split(part)
        return dot(jnp.concatenate([high, low, high], 1), table_y_ref[...])

    def along_x(part):
        high, low = split(part)
        return dot(table_x_ref[...], jnp.concatenate([high, high, low], 0))

    def quarters(part):
        return (
            part[:half_x, :half_y],
            part[:half_x, half_y:],
            part[half_x:, :half_y],
            part[half_x:, half_y:],
        )

    def join(ee, eo, oe, oo):
        return jnp.concatenate(
            [jnp.concatenate([ee, eo], 1), jnp.concatenate([oe, oo], 1)], 0
        )

    step = pl.program_id(0)

    @pl.when(step == 0)
    def to_planes():
        fetch(far_ref, phase_ref, sems)
        place = small_ref[steps : 2 * steps, :]
        for i, at in enumerate((lax.div(place, grid), lax.rem(place, grid))):
            place_ref[2 * i], place_ref[2 * i + 1] = folded(at)
        for k in range(planes):
            loaded = [got_ref[pl.ds(j, lines, stride=packs), k, :] for j in range(packs)]
            for part in range(2):
                spot = slice(part * columns, (part + 1) * columns)
                value = jnp.concatenate([v[:, spot] for v in loaded], 1)
                value = jnp.concatenate([value[:steps], value[steps:]], 1)
                for piece, half in enumerate(split(value)):
                    half = half.astype(f32)
                    value_ref[piece, 2 * (2 * k + part)] = half
                    value_ref[piece, 2 * (2 * k + part) + 1] = half * place_ref[1]
        field = jnp.zeros((count * size_x, size_y), f32)
        for q in range(steps):
            hot_x = ticks_x == place_ref[0, q : q + 1, :].astype(jnp.int32)
            hot_y = ticks_y == place_ref[2, q : q + 1, :].astype(jnp.int32)
            hot_y = jnp.concatenate(
                [jnp.where(hot_y, 1.0, 0.0), jnp.where(hot_y, place_ref[3, q : q + 1, :], 0.0)], 0
            ).astype(bf16)
            hot_ref[q] = hot_y
            for piece in range(2):
                spread = [
                    jnp.where(hot_x, value_ref[piece, i, q : q + 1, :], 0.0) for i in range(2 * count)
                ]
                field = field + dot(jnp.concatenate(spread, 0).astype(bf16), hot_y, 1, 1)
        field_ref[...] = field

    @pl.when(step == 1)
    def transforms():
        field = along_y(field_ref[...])
        back = []
        for k in range(planes):
            re, im = [
                quarters(along_x(field[(2 * k + i) * size_x : (2 * k + i + 1) * size_x]))
                for i in range(2)
            ]
            values_v = quarters(fold_ref[k])
            real_sum, real_gap = re[0] - re[3], re[0] + re[3]
            imag_sum, imag_gap = im[0] - im[3], im[0] + im[3]
            cross_re, cross_re_gap = re[1] + re[2], re[1] - re[2]
            cross_im, cross_im_gap = im[1] + im[2], im[1] - im[2]
            pp_re, mm_re = real_sum - cross_im, real_sum + cross_im
            pp_im, mm_im = imag_sum + cross_re, imag_sum - cross_re
            pm_re, mp_re = real_gap + cross_im_gap, real_gap - cross_im_gap
            pm_im, mp_im = imag_gap - cross_re_gap, imag_gap + cross_re_gap
            parts = []
            for pp, pm, mp, mm in (
                (pp_re, pm_re, mp_re, mm_re),
                (pp_im, pm_im, mp_im, mm_im),
            ):
                pp, pm, mp, mm = [a * b for a, b in zip((pp, pm, mp, mm), values_v)]
                plus_s, plus_g = pp + pm, pp - pm
                minus_s, minus_g = mp + mm, mp - mm
                parts.append((plus_s + minus_s, plus_g + minus_g, plus_s - minus_s, plus_g - minus_g))
            re, im = parts
            back.append(along_x(join(re[0], im[1], im[2], -re[3])))
            back.append(along_x(join(im[0], -re[1], -re[2], -im[3])))
        field_ref[...] = along_y(jnp.concatenate(back, 0))

    @pl.when(step == 2)
    def to_columns():
        high, low = split(field_ref[...])
        for q in range(steps):
            hot_x = ticks_x == place_ref[0, q : q + 1, :].astype(jnp.int32)
            sign_x = place_ref[1, q : q + 1, :]
            hot_y = hot_ref[q]
            mixed = dot(high, hot_y) + dot(low, hot_y)
            for i in range(count):
                even = mixed[i * size_x : i * size_x + half_x]
                odd = mixed[i * size_x + half_x : (i + 1) * size_x]
                picked = jnp.where(hot_x, even + sign_x * odd, 0.0)
                value_ref[0, i, q : q + 1, :] = jnp.sum(picked, 0, keepdims=True)
        for k in range(planes):
            halves = [value_ref[0, 2 * k + i] for i in range(2)]
            halves = [jnp.concatenate([v[:, :lanes], v[:, lanes:]], 0) for v in halves]
            ride = jnp.sum(got_ref[:, k, 2 * columns :], 0, keepdims=True)
            ride = jnp.broadcast_to(ride, (lines, ride.shape[1]))
            for j in range(packs):
                spot = slice(j * columns, (j + 1) * columns)
                send_ref[pl.ds(j, lines, stride=packs), k, :] = jnp.concatenate(
                    [halves[0][:, spot], halves[1][:, spot], ride], 1
                )
        for copy in make_copies(far_ref, phase_ref, sems):
            copy.wait()


def image_kernel(
    columns,
    waves,
    small_ref,
    form_ref,
    kinetic_ref,
    strength_ref,
    phase_ref,
    table_ref,
    psi_ref,
    got_ref,
    send_ref,
):
    groups, _, rows = phase_ref.shape
    atoms = phase_ref.shape[1] // 2
    grid = table_ref.shape[1]
    owners, planes, _ = got_ref.shape
    channels = form_ref.shape[0]
    root = math.sqrt(waves)
    got = [got_ref[:, k, :] for k in range(planes)]
    ride = [g[:, 2 * columns :] for g in got]
    wide = 2 * channels
    per_row = 2 * columns // wide
    sums = jnp.concatenate(
        [r[:, wide * i : wide * (i + 1)] for r in ride[:2] for i in range(per_row)], 0
    ).T
    line = lax.broadcasted_iota(jnp.int32, (wide, channels), 0)
    spot = lax.broadcasted_iota(jnp.int32, (wide, channels), 1)
    factor = jnp.sum(
        jnp.where(lax.rem(line, channels) == spot, strength_ref[...], 0.0), 1, keepdims=True
    )
    scaled = factor * (sums / root) / root
    scaled_re = scaled[:channels].astype(bf16)
    scaled_im = scaled[channels:].astype(bf16)
    first = jnp.concatenate([scaled_re, scaled_im], 0)
    second = jnp.concatenate([scaled_im, -scaled_re], 0)
    deep = split(jnp.concatenate([g[:, : 2 * columns] for g in got], 0).T)
    by_cos = dot3(deep, (table_ref[0], table_ref[1]))
    by_sin = dot3(deep, (table_ref[2], table_ref[3]))
    out_re = by_cos[:columns] + by_sin[columns:]
    out_im = by_cos[columns:] - by_sin[:columns]
    out = jnp.concatenate(split(jnp.concatenate([out_re, out_im], 0)), 0)
    ticks = lax.broadcasted_iota(jnp.int32, (columns, rows), 0)
    depths = lax.broadcasted_iota(jnp.int32, (grid, rows), 0)
    overlap = jnp.concatenate([ride[2][:, 0:4].T, ride[2][:, 4:8].T], 1)
    for s in range(groups):
        cell = small_ref[s : s + 1, :]
        depth_hot = (depths == lax.div(cell, columns)).astype(f32).astype(bf16)
        hot = ticks == lax.rem(cell, columns)
        found = dot(out, depth_hot)
        found = found[: 2 * columns] + found[2 * columns :]
        local_re = jnp.sum(jnp.where(hot, found[:columns], 0.0), 0, keepdims=True)
        local_im = jnp.sum(jnp.where(hot, found[columns:], 0.0), 0, keepdims=True)
        form = form_ref[:, s, :]
        mixed = dot(first, phase_ref[s, 0:atoms, :]) + dot(
            second, phase_ref[s, atoms : 2 * atoms, :]
        )
        near_re = jnp.sum(form * mixed[:channels], 0, keepdims=True)
        near_im = jnp.sum(form * mixed[channels:], 0, keepdims=True)
        kinetic = kinetic_ref[s : s + 1, :]
        image_re = kinetic * two_rows(psi_ref, s, 0) + local_re + near_re
        image_im = kinetic * two_rows(psi_ref, s, 2) + local_im + near_im
        send_ref[s, 0:1, :] = image_re[:, :128]
        send_ref[s, 1:2, :] = image_re[:, 128:]
        send_ref[s, 2:3, :] = image_im[:, :128]
        send_ref[s, 3:4, :] = image_im[:, 128:]
        send_ref[s, 4:8, :] = overlap


def overlap(waves, got_ref, over_ref):
    size = over_ref.shape[0] // 2
    packed = jnp.concatenate([got_ref[d, 4:8, :] for d in range(got_ref.shape[0])], 0)
    packed = unstripe(packed, 2) * (1.0 / waves)
    line = lax.broadcasted_iota(jnp.int32, (size, size), 0)
    spot = lax.broadcasted_iota(jnp.int32, (size, size), 1)
    turned = packed.T
    over_re = jnp.where(line <= spot, packed, turned)
    over_im = jnp.where(line < spot, -turned, jnp.where(line > spot, packed, 0.0))
    over_ref[...] = jnp.concatenate(
        [jnp.concatenate([over_re, -over_im], 1), jnp.concatenate([over_im, over_re], 1)], 0
    )


def products_kernel(waves, basis_ref, got_ref, image_ref, over_ref, send_ref):
    overlap(waves, got_ref, over_ref)
    bands = got_ref.shape[0]
    half = basis_ref.shape[0] // 2
    owners = send_ref.shape[0]
    image_re = jnp.concatenate([got_ref[:, 0, :], got_ref[:, 1, :]], 1)
    image_im = jnp.concatenate([got_ref[:, 2, :], got_ref[:, 3, :]], 1)
    image = jnp.concatenate([image_re, image_im], 0)
    image_ref[...] = image
    mixed = dot(image, basis_ref[...], 1, 1, exact_mode) * (1.0 / waves)
    coef_re = mixed[:bands, :half] + mixed[bands:, half:]
    coef_im = mixed[bands:, :half] - mixed[:bands, half:]
    coef = jnp.concatenate([coef_re, coef_im], 1)
    own = dot(image, image, 1, 1, exact_mode) * (1.0 / waves)
    own_re = own[:bands, :bands] + own[bands:, bands:]
    own_im = own[:bands, bands:] - own[bands:, :bands]
    line = lax.broadcasted_iota(jnp.int32, (bands, bands), 0)
    spot = lax.broadcasted_iota(jnp.int32, (bands, bands), 1)
    packed = jnp.where(line <= spot, own_re, own_im)
    row = jnp.concatenate(
        [stripes(coef, bands), stripes(packed, bands), jnp.zeros((1, 128 - bands * bands), f32)], 1
    )
    send_ref[:, 0, :] = jnp.broadcast_to(row, (owners, row.shape[1]))


def gather_kernel(got_ref, send_ref):
    row = jnp.sum(got_ref[:, 0, :], 0, keepdims=True)
    send_ref[:, 0, :] = jnp.broadcast_to(row, (send_ref.shape[0], row.shape[1]))


def finish_kernel(
    basis_ref, image_ref, over_ref, got_ref, next_re_ref, next_im_ref, coef_re_ref, coef_im_ref, chol_re_ref, chol_im_ref
):
    bands = image_ref.shape[0] // 2
    half = basis_ref.shape[0] // 2
    row = jnp.sum(got_ref[:, 0, :], 0, keepdims=True)
    size = bands * 2 * half
    coef = unstripe(row[:, :size], bands)
    packed = unstripe(row[:, size : size + bands * bands], bands)
    coef_re = coef[:, :half]
    coef_im = coef[:, half:]
    coef_re_ref[...] = coef_re.T
    coef_im_ref[...] = coef_im.T
    line = lax.broadcasted_iota(jnp.int32, (bands, bands), 0)
    spot = lax.broadcasted_iota(jnp.int32, (bands, bands), 1)
    turned = packed.T
    own_re = jnp.where(line <= spot, packed, turned)
    own_im = jnp.where(line < spot, -turned, jnp.where(line > spot, packed, 0.0))
    left = dot(coef, over_ref[...], 1, 0, exact_mode) - 2.0 * coef
    stacked = jnp.concatenate([coef, jnp.concatenate([-coef_im, coef_re], 1)], 0)
    mixed = dot(stacked, left, 1, 1, exact_mode)
    gram_re = own_re + mixed[:bands]
    gram_im = own_im + mixed[bands:]
    eye = jnp.where(line == spot, 1.0, 0.0)
    work_re = jnp.concatenate([gram_re, eye], 1)
    work_im = jnp.concatenate([gram_im, jnp.zeros_like(eye)], 1)
    rows_re, rows_im = [], []
    for k in range(bands):
        pivot = lax.rsqrt(work_re[k : k + 1, k : k + 1])
        lead_re = work_re[k : k + 1, :] * pivot
        lead_im = work_im[k : k + 1, :] * pivot
        rows_re.append(lead_re)
        rows_im.append(lead_im)
        if k + 1 < bands:
            column_re = work_re[:, k : k + 1] * pivot
            column_im = work_im[:, k : k + 1] * pivot
            work_re, work_im = (
                work_re - (column_re * lead_re - column_im * lead_im),
                work_im - (column_re * lead_im + column_im * lead_re),
            )
    all_re = jnp.concatenate(rows_re, 0)
    all_im = jnp.concatenate(rows_im, 0)
    chol_re_ref[...] = jnp.where(line <= spot, all_re[:, :bands], 0.0)
    chol_im_ref[...] = jnp.where(line < spot, all_im[:, :bands], 0.0)
    inv_re = all_re[:, bands:]
    inv_im = all_im[:, bands:]
    basis_re = basis_ref[0:half, :]
    basis_im = basis_ref[half : 2 * half, :]
    span_re = dot(coef, jnp.concatenate([basis_re, -basis_im], 0), 1, 0, exact_mode)
    span_im = dot(coef, jnp.concatenate([basis_im, basis_re], 0), 1, 0, exact_mode)
    rest_re = image_ref[0:bands, :] - span_re
    rest_im = image_ref[bands : 2 * bands, :] - span_im
    next_re = dot(inv_re, rest_re, 1, 0, exact_mode) + dot(inv_im, rest_im, 1, 0, exact_mode)
    next_im = dot(inv_re, rest_im, 1, 0, exact_mode) - dot(inv_im, rest_re, 1, 0, exact_mode)
    for ref, value in ((next_re_ref, next_re), (next_im_ref, next_im)):
        ref[pl.ds(0, bands, stride=2), :] = value[:, :128]
        ref[pl.ds(1, bands, stride=2), :] = value[:, 128:]


def body(
    basis_re,
    basis_im,
    potential,
    kinetic,
    form_factors,
    channel_strength,
    sphere_map,
    column_map,
    atom_sites,
):
    blocks, slab, _, row_count = basis_re.shape
    band_count = lax.axis_size("band")
    owners = lax.axis_size("pw")
    planes, grid, _ = potential.shape
    columns = column_map.shape[0] // owners
    waves = band_count * owners * row_count
    atoms = atom_sites.shape[1]
    rows = blocks * slab
    half_x, half_y = grid // 2 + 8, 128
    tables = transform_tables(grid, planes, half_x, half_y)
    owner_table, table_x, table_y = [jnp.asarray(table) for table in tables]

    def exchange(part, axis, groups=None):
        return lax.all_to_all(
            part, axis, split_axis=0, concat_axis=0, axis_index_groups=groups, tiled=True
        )

    near, far = {}, {}
    for z in range(band_count):
        for p in range(owners):
            y, rest = divmod(p, 8)
            near.setdefault((z // 2, y), []).append(z * owners + p)
            far.setdefault((z % 2, rest), []).append(z * owners + p)
    near, far = list(near.values()), list(far.values())

    places = column_map.reshape(-1, 128)
    basis, send, small = kernel_call(
        pack_kernel,
        (
            shape(2 * rows, row_count),
            shape(slab, 8, 128),
            shape(3 * 8, row_count, dtype=jnp.int32),
        ),
        basis_re.reshape(-1, 128),
        basis_im.reshape(-1, 128),
        sphere_map,
        places,
        atom_sites,
        scratch=(
            pltpu.VMEM((2 * rows, 128), f32),
            pltpu.VMEM((2 * rows, 128), f32),
            pltpu.VMEM(sphere_map.shape, jnp.int32),
            pltpu.VMEM(places.shape, jnp.int32),
            pltpu.VMEM(atom_sites.shape, jnp.int32),
            pltpu.SemaphoreType.DMA((2, 4)),
            pltpu.SemaphoreType.DMA((3,)),
        ),
        far=(0, 1, 2, 3, 4),
        vmem=63,
    )
    psi = exchange(send, "band")

    phase_dims = (band_count, 2 * atoms, row_count)
    first = band_count - 2
    phase_sems = (pltpu.SemaphoreType.DMA((band_count,)),)
    phase_scratch = (pltpu.VMEM(phase_dims, bf16),) + phase_sems
    far_phase = kernel_call(
        lambda *refs: phase_kernel(grid, columns, first, *refs),
        shape(16 * band_count, *phase_dims[1:], dtype=bf16),
        small,
        scratch=phase_scratch,
        far_out=(0,),
        vmem=8,
        flops=10**7,
    )
    send, folded, far_phase = kernel_call(
        lambda *refs: columns_kernel(columns, first, *refs),
        (
            shape(owners, planes, 128),
            shape(planes, 2 * half_x, 2 * half_y),
            shape(*far_phase.shape, dtype=bf16),
        ),
        small,
        form_factors,
        far_phase,
        owner_table,
        potential,
        psi,
        scratch=phase_scratch
        + (pltpu.VMEM((band_count, 16, row_count), bf16),) * 2,
        far=(2,),
        far_out=(2,),
        aliases={2: 2},
        grid=(3,),
    )
    got = exchange(send, "pw")
    send, phase = kernel_call(
        lambda *refs: planes_kernel(columns, grid, *refs),
        (shape(owners, planes, 128), shape(*phase_dims, dtype=bf16)),
        small,
        folded,
        table_x,
        table_y,
        far_phase,
        got,
        scratch=phase_sems
        + (
            pltpu.VMEM((2, 4 * planes, 8, row_count), f32),
            pltpu.VMEM((4, 8, row_count), f32),
            pltpu.VMEM((8, 2 * half_y, row_count), bf16),
            pltpu.VMEM((4 * planes * half_x, 2 * half_y), f32),
        ),
        grid=(3,),
        far=(4,),
        vmem=16,
    )
    got = exchange(send, "pw")
    send = kernel_call(
        lambda *refs: image_kernel(columns, waves, *refs),
        shape(band_count, 8, 128),
        small,
        form_factors,
        kinetic,
        channel_strength[None, :],
        phase,
        owner_table,
        psi,
        got,
    )
    got = exchange(send, "band")
    image, over, send = kernel_call(
        lambda *refs: products_kernel(waves, *refs),
        (
            shape(2 * slab, row_count),
            shape(2 * rows, 2 * rows),
            shape(len(near[0]), 1, 9 * 128),
        ),
        basis,
        got,
    )
    got = exchange(send, ("band", "pw"), near)
    send = kernel_call(gather_kernel, shape(len(far[0]), 1, 9 * 128), got)
    got = exchange(send, ("band", "pw"), far)
    next_re, next_im, coef_re, coef_im, chol_re, chol_im = kernel_call(
        finish_kernel,
        (
            shape(2 * slab, 128),
            shape(2 * slab, 128),
            shape(rows, slab),
            shape(rows, slab),
            shape(slab, slab),
            shape(slab, slab),
        ),
        basis,
        image,
        over,
        got,
    )
    return (
        next_re.reshape(slab, 1, row_count),
        next_im.reshape(slab, 1, row_count),
        coef_re.reshape(blocks, slab, slab),
        coef_im.reshape(blocks, slab, slab),
        chol_re,
        chol_im,
    )


def solution(mesh):
    return jax.shard_map(
        body,
        mesh=mesh,
        in_specs=(
            P(None, None, "band", "pw"),
            P(None, None, "band", "pw"),
            P("pw", None, None),
            P(None, "pw"),
            P(None, None, "pw"),
            P(),
            P(None, "pw"),
            P(),
            P(),
        ),
        out_specs=(P(None, "band", "pw"), P(None, "band", "pw"), P(), P(), P(), P()),
        check_vma=False,
    )
```
